256 devices in a mesh: tile: 32 (over y, z_hi, core), head: 8 (over z_lo, x).
Axes of the slice: x: 4, y: 4, z: 8 (z_hi: 4, z_lo: 2; z = z_hi * 2 + z_lo), core: 2. Of those that a mesh axis runs over, the one named last changes fastest.
Arguments:
- video_q: bfloat16 [16384, 3072], P('tile', 'head'), may hold values from -16 to 16
- video_k: bfloat16 [16384, 3072], P('tile', 'head'), may hold values from -16 to 16
- video_v: bfloat16 [16384, 3072], P('tile', 'head'), may hold values from -12 to 12
- text_q: bfloat16 [256, 3072], P('tile', 'head'), may hold values from -16 to 16
- text_k: bfloat16 [256, 3072], P('tile', 'head'), may hold values from -10 to 10
- text_v: bfloat16 [256, 3072], P('tile', 'head'), may hold values from -12 to 12
- video_proj: bfloat16 [3072, 3072], P('head'), may hold values from -0.109375 to 0.109375
- text_proj: bfloat16 [3072, 3072], P('head'), may hold values from -0.109375 to 0.109375
- window_mask: int32 [64, 27], P('tile'), may hold values from 0 to 1, as said below
- text_length: int32 [1], replicated, may hold values from 64 to 256
Outputs:
- video_out: bfloat16 [16384, 3072], P('tile', 'head')
- text_out: bfloat16 [256, 3072], P('tile', 'head')
The draws below stay inside these ranges and needn't reach their ends.
Inputs may be any that keep to these rules, and one draw needn't show every extreme that they name: window_mask[s, 9 a + 3 b + c] is 1 only if the tile at frame, row and column offsets a - 1, b - 1, c - 1 from tile s lies inside the grid of 2 x 4 x 8 tiles; the centre entry 13 is always 1.
All inputs are finite; a program needn't handle non-finite values.
Results may differ from the reference program's by a relative error of at most 0.013.
Values may be sent and summed in bfloat16 or wider, within the bound.
No kernel may reach another device: no remote copies, remote signals or barrier semaphores. Data moves between devices by JAX's collectives and lax.ppermute only.
A program may use at most 128 MiB of HBM per device.

```python
import math
import jax
import jax.numpy as jnp
from jax import lax

D = 3072
HEADS = 24
HD = 128
TILE_TOK = 256
TEXT = 256
GT = 2
BH = 1
BW = 1
DW = 8
GH = 4
GW = 8
TILES_DEV = 2
TILES = 64
VTOK = 16384
N_HEAD = 8


def base_rows(key, draw_tag, row_total):
    sub_key = jax.random.fold_in(key, draw_tag)
    return jnp.clip(1.4 * jax.random.normal(sub_key, (row_total, HEADS * HD), jnp.float32), -8.4, 8.4)


def drawn(key, draw_tag, row_total):
    values = base_rows(key, draw_tag, row_total)
    return values


def draw_video_q(key, part):
    return drawn(key, 11, VTOK).astype(jnp.bfloat16)


def draw_video_k(key, part):
    return drawn(key, 12, VTOK).astype(jnp.bfloat16)


def draw_text_q(key, part):
    return drawn(key, 13, TEXT).astype(jnp.bfloat16)


def draw_window_mask(key, part):
    slot_ids = jnp.arange(TILES, dtype=jnp.int32)
    device_ids = slot_ids // TILES_DEV
    local_ids = slot_ids % TILES_DEV
    frame_ids = local_ids // (BH * BW)
    row_ids = device_ids // DW * BH + local_ids // BW % BH
    col_ids = device_ids % DW * BW + local_ids % BW
    offset = jnp.arange(27, dtype=jnp.int32)
    near_frame = frame_ids[:, None] + offset[None, :] // 9 - 1
    near_row = row_ids[:, None] + offset[None, :] // 3 % 3 - 1
    near_col = col_ids[:, None] + offset[None, :] % 3 - 1
    inside = (near_frame >= 0) & (near_frame < GT) & (near_row >= 0) & (near_row < GH) & (near_col >= 0) & (near_col < GW)
    retained = jax.random.randint(jax.random.fold_in(key, 21), (TILES, 27), 0, 5) > 0
    return (inside & (retained | (offset == 13)[None, :])).astype(jnp.int32)


def block_scale(own_key, extent, pieces, low, top_value):
    factor_of = 1.0
    for axis_at, parts in pieces:
        steps = jax.random.uniform(jax.random.fold_in(jax.random.fold_in(own_key, 6), axis_at), (parts,), jnp.float32, low / len(pieces), top_value / len(pieces))
        factor_of = factor_of * jnp.repeat(jnp.exp(steps), extent[axis_at] // parts).reshape((-1,) + (1,) * (len(extent) - 1 - axis_at))
    return factor_of


def scatter_about(own_key, extent, scale, reach, cuts=(), kind=jnp.bfloat16):
    values = scale * jax.random.normal(own_key, extent, jnp.float32)
    if cuts:
        values = values * block_scale(own_key, extent, cuts, -0.22, 0.18)
    return jnp.clip(values, -reach, reach).astype(kind)


def setup_inputs(seed: int = 0) -> dict:
    keys = jax.random.split(jax.random.key(seed), 11)
    return {
        "video_q": draw_video_q(jax.random.fold_in(keys[10], 71), 0),
        "video_k": draw_video_k(jax.random.fold_in(keys[10], 71), 0),
        "video_v": scatter_about(keys[2], (VTOK, HEADS * HD), 2.0, 12.0, ((0, 32), (1, 8))),
        "text_q": draw_text_q(jax.random.fold_in(keys[10], 71), 0),
        "text_k": scatter_about(keys[4], (TEXT, HEADS * HD), 1.7, 10.0, ((0, 32), (1, 8))),
        "text_v": scatter_about(keys[5], (TEXT, HEADS * HD), 2.0, 12.0, ((0, 32), (1, 8))),
        "video_proj": scatter_about(keys[6], (HEADS * HD, D), (HEADS * HD) ** -0.5, 0.109375, ((0, 8),)),
        "text_proj": scatter_about(keys[7], (HEADS * HD, D), (HEADS * HD) ** -0.5, 0.109375, ((0, 8),)),
        "window_mask": draw_window_mask(jax.random.fold_in(keys[10], 71), 0),
        "text_length": jax.random.randint(keys[9], (1,), TEXT // 4, TEXT + 1).astype(jnp.int32),
    }


NEG_FILL = -1e+30

def attend_tile(queries, window_keys, window_values, key_live, text_keys, text_values, text_live, score_scale):
    near_scores = jnp.einsum('qhd,khd->hqk', queries.astype(jnp.float32), window_keys.astype(jnp.float32)) * score_scale
    near_scores = jnp.where(key_live[None, None, :], near_scores, NEG_FILL)
    text_scores = jnp.einsum('qhd,khd->hqk', queries.astype(jnp.float32), text_keys.astype(jnp.float32)) * score_scale
    text_scores = jnp.where(text_live[None, None, :], text_scores, NEG_FILL)
    row_peak = jnp.maximum(lax.optimization_barrier(jnp.max(near_scores, axis=-1)), lax.optimization_barrier(jnp.max(text_scores, axis=-1)))
    near_weights = jnp.exp(near_scores - row_peak[..., None])
    text_weights = jnp.exp(text_scores - row_peak[..., None])
    weight_sum = lax.optimization_barrier(jnp.sum(near_weights, axis=-1)) + lax.optimization_barrier(jnp.sum(text_weights, axis=-1))
    near_rounded = lax.optimization_barrier(near_weights.astype(jnp.bfloat16)).astype(jnp.float32)
    text_rounded = lax.optimization_barrier(text_weights.astype(jnp.bfloat16)).astype(jnp.float32)
    weighted = jnp.einsum('hqk,khd->hqd', near_rounded, window_values.astype(jnp.float32))
    weighted = weighted + jnp.einsum('hqk,khd->hqd', text_rounded, text_values.astype(jnp.float32))
    result = weighted / weight_sum[..., None]
    return jnp.transpose(result, (1, 0, 2)).reshape(queries.shape[0], -1).astype(jnp.bfloat16)

def project_groups(attended, weight):
    row_total = attended.shape[0]
    group_width = attended.shape[1] // N_HEAD
    grouped = jnp.transpose(attended.reshape(row_total, N_HEAD, group_width), (1, 0, 2))
    weight_groups = weight.reshape(N_HEAD, group_width, weight.shape[1])

    def add_group(running_sum, group_pair):
        partial_sum = jnp.dot(group_pair[0], group_pair[1], preferred_element_type=jnp.float32).astype(jnp.bfloat16)
        partial_sum = lax.optimization_barrier(partial_sum)
        return (running_sum + partial_sum.astype(jnp.float32), None)
    running_sum, unused_out = lax.scan(add_group, jnp.zeros((row_total, weight.shape[1]), jnp.float32), (grouped, weight_groups))
    return running_sum.astype(jnp.bfloat16)

def reference(video_q, video_k, video_v, text_q, text_k, text_v, video_proj, text_proj, window_mask, text_length):
    score_scale = 1.0 / math.sqrt(HD)
    slot_ids = jnp.arange(TILES, dtype=jnp.int32)
    device_ids = slot_ids // TILES_DEV
    local_ids = slot_ids % TILES_DEV
    frame_ids = local_ids // (BH * BW)
    row_ids = device_ids // DW * BH + local_ids // BW % BH
    col_ids = device_ids % DW * BW + local_ids % BW
    offsets = jnp.arange(3, dtype=jnp.int32) - 1
    frame_grid = jnp.broadcast_to(jnp.arange(GT, dtype=jnp.int32)[None, :, None, None], (TILES, GT, 3, 3))
    row_grid = jnp.broadcast_to(jnp.clip(row_ids[:, None, None, None] + offsets[None, None, :, None], 0, GH - 1), (TILES, GT, 3, 3))
    col_grid = jnp.broadcast_to(jnp.clip(col_ids[:, None, None, None] + offsets[None, None, None, :], 0, GW - 1), (TILES, GT, 3, 3))
    neighbour_slots = (row_grid // BH * DW + col_grid // BW) * TILES_DEV + (frame_grid * BH + row_grid % BH) * BW + col_grid % BW
    neighbour_slots = neighbour_slots.reshape(TILES, GT * 9).astype(jnp.int32)
    frame_gap = frame_grid - frame_ids[:, None, None, None] + 1
    mask_column = jnp.clip(frame_gap, 0, 2) * 9 + jnp.broadcast_to((offsets[None, None, :, None] + 1) * 3 + offsets[None, None, None, :] + 1, (TILES, GT, 3, 3))
    mask_column = mask_column.reshape(TILES, GT * 9).astype(jnp.int32)
    tile_live = (jnp.take_along_axis(window_mask, mask_column, axis=1) > 0) & (jnp.abs(frame_gap - 1) <= 1).reshape(TILES, GT * 9)
    tiled_keys = video_k.reshape(TILES, TILE_TOK, HEADS, HD)
    tiled_values = video_v.reshape(TILES, TILE_TOK, HEADS, HD)
    tiled_queries = video_q.reshape(TILES, TILE_TOK, HEADS, HD)
    text_keys = text_k.reshape(TEXT, HEADS, HD)
    text_values = text_v.reshape(TEXT, HEADS, HD)
    text_live = jnp.arange(TEXT, dtype=jnp.int32) < text_length[0]

    def one_tile(slot_index):
        near_keys = tiled_keys[neighbour_slots[slot_index]].reshape(GT * 9 * TILE_TOK, HEADS, HD)
        near_values = tiled_values[neighbour_slots[slot_index]].reshape(GT * 9 * TILE_TOK, HEADS, HD)
        key_live = jnp.repeat(tile_live[slot_index], TILE_TOK)
        return attend_tile(tiled_queries[slot_index], near_keys, near_values, key_live, text_keys, text_values, text_live, score_scale)
    video_attn = lax.map(one_tile, slot_ids).reshape(VTOK, HEADS * HD)

    def head_major(array, count):
        return jnp.transpose(array.reshape(count, HEADS, HD), (1, 0, 2))

    def one_head(head_parts):
        head_query, head_keys, head_values, head_text_keys, head_text_values = head_parts
        near_scores = jnp.dot(head_query, head_keys.T, preferred_element_type=jnp.float32) * score_scale
        text_scores = jnp.dot(head_query, head_text_keys.T, preferred_element_type=jnp.float32) * score_scale
        text_scores = jnp.where(text_live[None, :], text_scores, NEG_FILL)
        row_peak = jnp.maximum(lax.optimization_barrier(jnp.max(near_scores, axis=-1)), lax.optimization_barrier(jnp.max(text_scores, axis=-1)))
        near_weights = jnp.exp(near_scores - row_peak[:, None])
        text_weights = jnp.exp(text_scores - row_peak[:, None])
        weight_sum = lax.optimization_barrier(jnp.sum(near_weights, axis=-1)) + lax.optimization_barrier(jnp.sum(text_weights, axis=-1))
        weighted = jnp.dot(near_weights, head_values.astype(jnp.float32), precision=lax.Precision.HIGHEST)
        weighted = weighted + jnp.dot(text_weights, head_text_values.astype(jnp.float32), precision=lax.Precision.HIGHEST)
        return weighted / weight_sum[:, None]
    text_heads = lax.map(one_head, (head_major(text_q, TEXT), head_major(video_k, VTOK), head_major(video_v, VTOK), head_major(text_k, TEXT), head_major(text_v, TEXT)))
    text_attn = jnp.transpose(text_heads, (1, 0, 2)).reshape(TEXT, HEADS * HD).astype(jnp.bfloat16)
    return (project_groups(video_attn, video_proj), project_groups(text_attn, text_proj))
```

```python
import functools
import math

import jax
import jax.numpy as jnp
from jax import lax
from jax.experimental import pallas as pl
from jax.experimental.pallas import tpu as pltpu
from jax.sharding import PartitionSpec as P

HD = 128
TT = 256
NH = 3
W = NH * HD
TEXT = 256
TL = 8
ROWS = 2 * TT
SCALE = math.log2(math.e) / math.sqrt(HD)
BIG = 1e30
F32 = jnp.float32
BF16 = jnp.bfloat16

ANY = pl.BlockSpec(memory_space=pl.ANY)
SM = pl.BlockSpec(memory_space=pltpu.SMEM)
VM = pl.BlockSpec(memory_space=pltpu.VMEM)


def params(mib):
    return pltpu.CompilerParams(vmem_limit_bytes=mib * 2**20)


def cost(flops, nbytes, exps=0):
    return pl.CostEstimate(flops=flops, bytes_accessed=nbytes, transcendentals=exps)


def rows_on(x, d):
    return lax.ppermute(x, "tile", [(i, ((i // 8 + d) % 4) * 8 + i % 8) for i in range(32)])


def over_chip(x):
    return lax.ppermute(
        x, "tile", [(i, (i // 8) * 8 + (i % 8 + (1 if i % 2 else -1)) % 8) for i in range(32)]
    )


def other_core(x):
    return lax.ppermute(x, "tile", [(i, i ^ 1) for i in range(32)])


def x_on(x, d):
    return lax.ppermute(x, "head", [(i, (i // 4) * 4 + (i + d) % 4) for i in range(8)])


def z_pair(x):
    return lax.ppermute(x, "head", [(i, i ^ 4) for i in range(8)])


def fold(x, op):
    r = x[:, :HD]
    for i in range(1, x.shape[1] // HD):
        r = op(r, x[:, i * HD : (i + 1) * HD])
    return r


def scores(q, k):
    return lax.dot_general(q, k, (((1,), (1,)), ((), ())), preferred_element_type=F32)


def spread(col):
    return jnp.broadcast_to(col, (col.shape[0], HD))


def bias_of(wm, tile, frame, row, col):
    live = wm[tile, 9 * (frame - tile + 1) + 3 * row + col]
    return jnp.where(live > 0, 0.0, -BIG).astype(F32)


def early_kernel(
    wm, tlen, core, q_ref, tk_ref, tv_ref, b0, b1, b2, b3, b4, b5,
    acc_ref, m_ref, l_ref, kbuf, s_s, mx_s, sem,
):
    blocks = (b0, b1, b2, b3, b4, b5)
    nb = len(blocks)
    for b in range(nb):
        pltpu.make_async_copy(blocks[b], kbuf.at[b], sem.at[b]).start()
    lane = lax.broadcasted_iota(jnp.int32, (1, TEXT), 1)
    tbias = jnp.where(lane < tlen[0], 0.0, -BIG)
    pcol = jnp.where(core[0] == 0, 2, 0)
    colof = (1, 1, 1, pcol, pcol, pcol)
    rowof = (1, 0, 2, 1, 0, 2)

    def hs(h):
        return pl.ds(h * HD, HD)

    def p1_text(h, w):
        for t in range(2):
            s = scores(q_ref[pl.ds(t * TT, TT), hs(h)], tk_ref[:, hs(h)]) * SCALE + tbias
            s_s[w, t, nb, :, :TEXT] = s
            mx_s[w, t] = fold(s, jnp.maximum)

    def p1(h, w, b):
        k = kbuf[b, :ROWS, hs(h)]
        for t in range(2):
            s = scores(q_ref[pl.ds(t * TT, TT), hs(h)], k)
            mx = mx_s[w, t]
            for f in range(2):
                sf = s[:, f * TT : (f + 1) * TT] * SCALE + bias_of(wm, t, f, rowof[b], colof[b])
                s_s[w, t, b, :, f * TT : (f + 1) * TT] = sf
                mx = jnp.maximum(mx, fold(sf, jnp.maximum))
            mx_s[w, t] = mx

    def top(h, w):
        for t in range(2):
            m_ref[pl.ds(t * TT, TT), hs(h)] = spread(jnp.max(mx_s[w, t], axis=1, keepdims=True))

    def weigh(s, m):
        return jnp.concatenate(
            [jnp.exp2(s[:, i * HD : (i + 1) * HD] - m) for i in range(s.shape[1] // HD)], axis=1
        )

    def p2_text(h, w):
        for t in range(2):
            rs = pl.ds(t * TT, TT)
            p = weigh(s_s[w, t, nb, :, :TEXT], m_ref[rs, hs(h)])
            l_ref[rs, hs(h)] = fold(p, jnp.add)
            acc_ref[rs, hs(h)] = jnp.dot(
                p.astype(BF16), tv_ref[:, hs(h)], preferred_element_type=F32
            )

    def p2(h, w, b):
        v = kbuf[b, ROWS:, hs(h)]
        for t in range(2):
            rs = pl.ds(t * TT, TT)
            p = weigh(s_s[w, t, b], m_ref[rs, hs(h)])
            l_ref[rs, hs(h)] += fold(p, jnp.add)
            acc_ref[rs, hs(h)] += jnp.dot(p.astype(BF16), v, preferred_element_type=F32)

    p1_text(0, 0)
    for b in range(nb):
        pltpu.make_async_copy(blocks[b], kbuf.at[b], sem.at[b]).wait()
        p1(0, 0, b)
    top(0, 0)
    for h in range(NH):
        w = h % 2
        p2_text(h, w)
        if h + 1 < NH:
            p1_text(h + 1, 1 - w)
        for b in range(nb):
            p2(h, w, b)
            if h + 1 < NH:
                p1(h + 1, 1 - w, b)
        if h + 1 < NH:
            top(h + 1, 1 - w)


def early(wm, tlen, core, q, tk, tv, blocks):
    nb = len(blocks)
    part = jax.ShapeDtypeStruct((ROWS, W), F32)
    return pl.pallas_call(
        early_kernel,
        out_shape=(part, part, part),
        in_specs=[SM, SM, SM, VM, VM, VM] + [ANY] * nb,
        out_specs=(VM, VM, VM),
        scratch_shapes=[
            pltpu.VMEM((nb, 2 * ROWS, W), BF16),
            pltpu.VMEM((2, 2, nb + 1, TT, ROWS), F32),
            pltpu.VMEM((2, 2, TT, HD), F32),
            pltpu.SemaphoreType.DMA((nb,)),
        ],
        compiler_params=params(44),
        cost_estimate=cost(4 * ROWS * (nb * ROWS + TEXT) * W, 8 * 2**20, ROWS * nb * ROWS * NH),
        name="early",
    )(wm, tlen, core, q, tk, tv, *blocks)


def late_kernel(wm, core, q_ref, b0, b1, b2, acc_ref, m_ref, l_ref, o_ref):
    blocks = (b0, b1, b2)
    fcol = jnp.where(core[0] == 0, 0, 2)
    rowof = (1, 0, 2)
    for t in range(2):
        rs = pl.ds(t * TT, TT)
        parts = []
        mx = None
        for b in range(3):
            s = scores(q_ref[rs, :], blocks[b][:ROWS, :])
            for f in range(2):
                sf = s[:, f * TT : (f + 1) * TT] * SCALE + bias_of(wm, t, f, rowof[b], fcol)
                parts.append(sf)
                fx = fold(sf, jnp.maximum)
                mx = fx if mx is None else jnp.maximum(mx, fx)
        mo = m_ref[rs, :]
        mn = jnp.maximum(mo, spread(jnp.max(mx, axis=1, keepdims=True)))
        al = jnp.exp2(mo - mn)
        acc = acc_ref[rs, :] * al
        tot = l_ref[rs, :] * al
        for b in range(3):
            p = jnp.concatenate(
                [
                    jnp.exp2(parts[2 * b + f][:, i * HD : (i + 1) * HD] - mn)
                    for f in range(2)
                    for i in range(2)
                ],
                axis=1,
            )
            tot += fold(p, jnp.add)
            acc += jnp.dot(p.astype(BF16), blocks[b][ROWS:, :], preferred_element_type=F32)
        o_ref[rs, :] = (acc / jnp.sum(tot, axis=1, keepdims=True)).astype(BF16)


def late(h, wm, core, q, far, far_up, far_dn, acc, m, l):
    head = pl.BlockSpec((ROWS, HD), lambda i: (0, h))
    block = pl.BlockSpec((2 * ROWS, HD), lambda i: (0, h))
    own = pl.BlockSpec((2 * ROWS, HD), lambda i: (0, 0))
    return pl.pallas_call(
        late_kernel,
        grid=(1,),
        out_shape=jax.ShapeDtypeStruct((ROWS, HD), BF16),
        in_specs=[SM, SM, head, block, own, own, head, head, head],
        out_specs=pl.BlockSpec((ROWS, HD), lambda i: (0, 0)),
        compiler_params=params(32),
        cost_estimate=cost(12 * ROWS * ROWS * HD, 2 * 2**20, 3 * ROWS * ROWS),
        name="late",
    )(wm, core, q, far, far_up, far_dn, acc, m, l)


def pieces3(x):
    hi = x.astype(BF16).astype(F32)
    mid = (x - hi).astype(BF16).astype(F32)
    return hi, mid, x - hi - mid


def text_kernel(tq_ref, kv_ref, msg_ref):
    lane = lax.broadcasted_iota(jnp.int32, (TEXT, HD), 1)
    stat = jnp.zeros((TEXT, HD), F32)
    for h in range(NH):
        hs = pl.ds(h * HD, HD)
        s = scores(tq_ref[:, hs], kv_ref[:ROWS, hs]) * SCALE
        m = jnp.max(fold(s, jnp.maximum), axis=1, keepdims=True)
        p = jnp.exp2(s - m)
        tot = jnp.sum(fold(p, jnp.add), axis=1, keepdims=True)
        acc = jnp.dot(p.astype(BF16), kv_ref[ROWS:, hs], preferred_element_type=F32)
        msg_ref[:, hs] = (acc / tot).astype(BF16)
        for j, piece in enumerate(pieces3(m + jnp.log2(tot))):
            stat = jnp.where(lane == 8 * j + h, spread(piece), stat)
    msg_ref[:, W:] = stat.astype(BF16)


def text_part(tq, kv):
    return pl.pallas_call(
        text_kernel,
        out_shape=jax.ShapeDtypeStruct((TEXT, W + HD), BF16),
        in_specs=[VM, VM],
        out_specs=VM,
        compiler_params=params(24),
        cost_estimate=cost(4 * TEXT * ROWS * W, 2 * 2**20, TEXT * ROWS * NH),
        name="text_part",
    )(tq, kv)


def merge_kernel(tlen, at, msg_ref, tq_ref, tk_ref, tv_ref, proj_ref, out_ref, flat):
    msg = msg_ref[...].astype(F32)
    stat = msg[:, W:]
    slane = lax.broadcasted_iota(jnp.int32, (TEXT, HD), 1)
    lane = lax.broadcasted_iota(jnp.int32, (1, TEXT), 1)
    tbias = jnp.where(lane < tlen[0], 0.0, -BIG)
    q = tq_ref[...]
    attn = []
    for h in range(NH):
        hs = slice(h * HD, (h + 1) * HD)
        s = scores(q[:, hs], tk_ref[:, hs]) * SCALE + tbias
        m = jnp.max(s, axis=1, keepdims=True)
        p = jnp.exp2(s - m)
        tot = jnp.sum(p, axis=1, keepdims=True)
        own = jnp.dot(p.astype(BF16), tv_ref[:, hs], preferred_element_type=F32)
        mine = (slane == h) | (slane == 8 + h) | (slane == 16 + h)
        lse = jnp.sum(jnp.where(mine, stat, 0.0), axis=1, keepdims=True)
        lse = spread(lse).reshape(TEXT // TL, TL, HD)
        peak = jnp.maximum(jnp.max(lse, axis=0), spread(m))
        wt = jnp.exp2(lse - peak[None])
        w0 = jnp.exp2(spread(m) - peak)
        num = jnp.sum(wt * msg[:, hs].reshape(TEXT // TL, TL, HD), axis=0) + w0 * own
        den = jnp.sum(wt, axis=0) + w0 * tot
        attn.append((num / den).astype(BF16))
    a = jnp.concatenate(attn, axis=1)
    flat[...] = jnp.dot(a, proj_ref[...], preferred_element_type=F32)
    x, z = at[0], at[1]
    for s in range(4):
        xd = lax.rem(x + s, 4)
        for j in range(2):
            zd = z if j == 0 else 1 - z
            col = pl.multiple_of((zd * 4 + xd) * W, HD)
            out_ref[s, :, j * W : (j + 1) * W] = flat[:, pl.ds(col, W)].astype(BF16)


def text_merge(tlen, at, msg, tq, tk, tv, proj):
    return pl.pallas_call(
        merge_kernel,
        out_shape=jax.ShapeDtypeStruct((4, TL, 2 * W), BF16),
        in_specs=[SM, SM, VM, VM, VM, VM, VM],
        out_specs=VM,
        scratch_shapes=[pltpu.VMEM((TL, 8 * W), F32)],
        compiler_params=params(24),
        cost_estimate=cost(2 * TL * W * 8 * W, 3 * 2**20, TEXT * HD * NH),
        name="text_merge",
    )(tlen, at, msg, tq, tk, tv, proj)


def split_kernel(at, proj_ref, o0, o1, o2, o3, sem):
    x, z = at[0], at[1]
    copies = []
    for s, out in enumerate((o0, o1, o2, o3)):
        xd = lax.rem(x + s, 4)
        for j in range(2):
            zd = z if j == 0 else 1 - z
            col = pl.multiple_of((zd * 4 + xd) * W, HD)
            copies.append(
                pltpu.make_async_copy(
                    proj_ref.at[:, pl.ds(col, W)], out.at[:, pl.ds(j * W, W)], sem.at[2 * s + j]
                )
            )
    for c in copies:
        c.start()
    for c in copies:
        c.wait()


def split_proj(at, proj):
    piece = jax.ShapeDtypeStruct((W, 2 * W), BF16)
    return pl.pallas_call(
        split_kernel,
        out_shape=(piece,) * 4,
        in_specs=[SM, ANY],
        out_specs=(ANY,) * 4,
        scratch_shapes=[pltpu.SemaphoreType.DMA((8,))],
        cost_estimate=cost(0, 5 * 2**20),
        name="split_proj",
    )(at, proj)


def project_kernel(*refs):
    a_refs, w_refs, t_refs = refs[:12], refs[12:16], refs[16:20]
    own_ref, away_ref = refs[20:]
    w = jnp.concatenate([r[...] for r in w_refs], axis=0)
    for i in range(2):
        rs = pl.ds(i * TT, TT)
        a = jnp.concatenate([r[rs, :] for r in a_refs], axis=1)
        o = jnp.dot(a, w, preferred_element_type=F32)
        own_ref[rs, :] = o[:, :W]
        away_ref[rs, :] = o[:, W:].astype(BF16)
    t = t_refs[0][...].astype(F32)
    for r in t_refs[1:]:
        t += r[...].astype(F32)
    t = jnp.concatenate([t, jnp.zeros_like(t)], axis=0)
    own_ref[pl.ds(ROWS, 16), :] = t[:, :W]
    away_ref[pl.ds(ROWS, 16), :] = t[:, W:].astype(BF16)


def project(attn, proj, text):
    return pl.pallas_call(
        project_kernel,
        out_shape=(
            jax.ShapeDtypeStruct((ROWS + 16, W), F32),
            jax.ShapeDtypeStruct((ROWS + 16, W), BF16),
        ),
        in_specs=[VM] * 20,
        out_specs=(VM, VM),
        compiler_params=params(32),
        cost_estimate=cost(2 * ROWS * 4 * W * 2 * W, 6 * 2**20),
        name="project",
    )(*attn, *proj, *text)


def add_kernel(own_ref, got_ref, video_ref, text_ref):
    video_ref[...] = (own_ref[:ROWS, :] + got_ref[:ROWS, :].astype(F32)).astype(BF16)
    t = own_ref[pl.ds(ROWS, 16), :] + got_ref[pl.ds(ROWS, 16), :].astype(F32)
    text_ref[...] = t[:TL, :].astype(BF16)


def add_up(own, got):
    return pl.pallas_call(
        add_kernel,
        out_shape=(jax.ShapeDtypeStruct((ROWS, W), BF16), jax.ShapeDtypeStruct((TL, W), BF16)),
        in_specs=[VM, VM],
        out_specs=(VM, VM),
        cost_estimate=cost(0, 2 * 2**20),
        name="add_up",
    )(own, got)


def per_device(
    video_q, video_k, video_v, text_q, text_k, text_v, video_proj, text_proj, window_mask, text_length
):
    core = (lax.axis_index("tile") % 2).astype(jnp.int32).reshape(1)
    head_at = lax.axis_index("head").astype(jnp.int32)
    at = jnp.stack([head_at % 4, head_at // 4])

    kv = jnp.concatenate([video_k, video_v], axis=0)
    far = over_chip(kv)
    up = rows_on(kv, 1)
    dn = rows_on(kv, -1)
    side = other_core(kv)

    both = jnp.concatenate([text_q, text_k, text_v], axis=1)
    every = lax.all_to_all(
        jnp.broadcast_to(both[None], (32, *both.shape)), "tile", 0, 0, tiled=True
    ).reshape(TEXT, 3 * W)
    tq, tk, tv = every[:, :W], every[:, W : 2 * W], every[:, 2 * W :]

    pieces = split_proj(at, video_proj)
    proj = [pieces[0]] + [x_on(pieces[s], s) for s in range(1, 4)]

    msg = text_part(tq, kv).reshape(32, TL, W + HD)

    far_up, far_dn = [], []
    for h in range(NH):
        fh = far[:, h * HD : (h + 1) * HD]
        far_up.append(rows_on(fh, 1))
        far_dn.append(rows_on(fh, -1))
    side_up, side_dn = other_core(up), other_core(dn)

    acc, m, l = early(
        window_mask, text_length, core, video_q, tk, tv, (kv, up, dn, side, side_up, side_dn)
    )
    got = lax.all_to_all(msg, "tile", 0, 0, tiled=True).reshape(TEXT, W + HD)

    attn = []
    for h in range(NH):
        a = late(h, window_mask, core, video_q, far, far_up[h], far_dn[h], acc, m, l)
        attn.append([a] + [x_on(a, s) for s in range(1, 4)])

    tp = text_merge(text_length, at, got, text_q, tk, tv, text_proj)
    text = [tp[0]] + [x_on(tp[s], s) for s in range(1, 4)]

    own, away = project([attn[h][s] for s in range(4) for h in range(NH)], proj, text)
    return add_up(own, z_pair(away))


def solution(mesh):
    both, rows = P("tile", "head"), P("head", None)
    return jax.shard_map(
        per_device,
        mesh=mesh,
        in_specs=(both,) * 6 + (rows, rows, P("tile", None), P()),
        out_specs=(both, both),
        check_vma=False,
    )
```

```python
import functools
import math

import jax
import jax.numpy as jnp
from jax import lax
from jax.experimental import pallas as pl
from jax.experimental.pallas import tpu as pltpu
from jax.sharding import PartitionSpec as P

HD = 128
TT = 256
NH = 3
W = NH * HD
TEXT = 256
TL = 8
ROWS = 2 * TT
SCALE = math.log2(math.e) / math.sqrt(HD)
BIG = 1e30
F32 = jnp.float32
BF16 = jnp.bfloat16

ANY = pl.BlockSpec(memory_space=pl.ANY)
SM = pl.BlockSpec(memory_space=pltpu.SMEM)
VM = pl.BlockSpec(memory_space=pltpu.VMEM)
HBM = pl.BlockSpec(memory_space=pltpu.HBM)


def params(mib):
    return pltpu.CompilerParams(vmem_limit_bytes=mib * 2**20)


def cost(flops, nbytes, exps=0):
    return pl.CostEstimate(flops=1, bytes_accessed=1, transcendentals=1)


def rows_on(x, d):
    return lax.ppermute(x, "tile", [(i, ((i // 8 + d) % 4) * 8 + i % 8) for i in range(32)])


def over_chip(x):
    return lax.ppermute(
        x, "tile", [(i, (i // 8) * 8 + (i % 8 + (1 if i % 2 else -1)) % 8) for i in range(32)]
    )


def other_core(x):
    return lax.ppermute(x, "tile", [(i, i ^ 1) for i in range(32)])


def x_swap(x):
    groups = [[0, 1, 2, 3], [4, 5, 6, 7]]
    return lax.all_to_all(x, "head", 0, 0, tiled=True, axis_index_groups=groups)


def x_on(x, d):
    return lax.ppermute(x, "head", [(i, (i // 4) * 4 + (i + d) % 4) for i in range(8)])


def z_pair(x):
    return lax.ppermute(x, "head", [(i, i ^ 4) for i in range(8)])


def fold(x, op):
    r = x[:, :HD]
    for i in range(1, x.shape[1] // HD):
        r = op(r, x[:, i * HD : (i + 1) * HD])
    return r


def scores(q, k):
    return lax.dot_general(q, k, (((1,), (1,)), ((), ())), preferred_element_type=F32)


def spread(col):
    return jnp.broadcast_to(col, (col.shape[0], HD))


def bias_of(wm, tile, frame, row, col):
    live = wm[tile, 9 * (frame - tile + 1) + 3 * row + col]
    return jnp.where(live > 0, 0.0, -BIG).astype(F32)


def early_kernel(
    wm, tlen, q_ref, t_ref, b0, b1, b2, b3, b4, b5, acc_ref, m_ref, l_ref, kbuf, s_s, mx_s, sem
):
    blocks = (b0, b1, b2, b3, b4, b5)
    nb = len(blocks)
    for b in range(nb):
        pltpu.make_async_copy(blocks[b], kbuf.at[b], sem.at[b]).start()
    lane = lax.broadcasted_iota(jnp.int32, (1, TEXT), 1)
    tbias = jnp.where(lane < tlen[0], 0.0, -BIG)
    pcol = 2 - 2 * lax.rem(lax.axis_index("tile"), 2)
    colof = (1, 1, 1, pcol, pcol, pcol)
    rowof = (1, 0, 2, 1, 0, 2)

    def hs(h):
        return pl.ds(h * HD, HD)

    def p1_text(h, w):
        for t in range(2):
            k = t_ref[:, pl.ds(W + h * HD, HD)]
            s = scores(q_ref[pl.ds(t * TT, TT), hs(h)], k) * SCALE + tbias
            s_s[w, t, nb, :, :TEXT] = s
            mx_s[w, t] = fold(s, jnp.maximum)

    def p1(h, w, b):
        k = kbuf[b, :ROWS, hs(h)]
        for t in range(2):
            s = scores(q_ref[pl.ds(t * TT, TT), hs(h)], k)
            mx = mx_s[w, t]
            for f in range(2):
                sf = s[:, f * TT : (f + 1) * TT] * SCALE + bias_of(wm, t, f, rowof[b], colof[b])
                s_s[w, t, b, :, f * TT : (f + 1) * TT] = sf
                mx = jnp.maximum(mx, fold(sf, jnp.maximum))
            mx_s[w, t] = mx

    def top(h, w):
        for t in range(2):
            m_ref[pl.ds(t * TT, TT), hs(h)] = spread(jnp.max(mx_s[w, t], axis=1, keepdims=True))

    def weigh(s, m):
        return jnp.concatenate(
            [jnp.exp2(s[:, i * HD : (i + 1) * HD] - m) for i in range(s.shape[1] // HD)], axis=1
        )

    def p2_text(h, w):
        for t in range(2):
            rs = pl.ds(t * TT, TT)
            p = weigh(s_s[w, t, nb, :, :TEXT], m_ref[rs, hs(h)])
            l_ref[rs, hs(h)] = fold(p, jnp.add)
            v = t_ref[:, pl.ds(2 * W + h * HD, HD)]
            acc_ref[rs, hs(h)] = jnp.dot(p.astype(BF16), v, preferred_element_type=F32)

    def p2(h, w, b):
        v = kbuf[b, ROWS:, hs(h)]
        for t in range(2):
            rs = pl.ds(t * TT, TT)
            p = weigh(s_s[w, t, b], m_ref[rs, hs(h)])
            l_ref[rs, hs(h)] += fold(p, jnp.add)
            acc_ref[rs, hs(h)] += jnp.dot(p.astype(BF16), v, preferred_element_type=F32)

    p1_text(0, 0)
    for b in range(nb):
        pltpu.make_async_copy(blocks[b], kbuf.at[b], sem.at[b]).wait()
        p1(0, 0, b)
    top(0, 0)
    for h in range(NH):
        w = h % 2
        p2_text(h, w)
        if h + 1 < NH:
            p1_text(h + 1, 1 - w)
        for b in range(nb):
            p2(h, w, b)
            if h + 1 < NH:
                p1(h + 1, 1 - w, b)
        if h + 1 < NH:
            top(h + 1, 1 - w)


def early(wm, tlen, q, every, blocks):
    nb = len(blocks)
    part = jax.ShapeDtypeStruct((ROWS, W), F32)
    return pl.pallas_call(
        early_kernel,
        out_shape=(part, part, part),
        in_specs=[SM, SM, VM, VM] + [ANY] * nb,
        out_specs=(VM, VM, VM),
        scratch_shapes=[
            pltpu.VMEM((nb, 2 * ROWS, W), BF16),
            pltpu.VMEM((2, 2, nb + 1, TT, ROWS), F32),
            pltpu.VMEM((2, 2, TT, HD), F32),
            pltpu.SemaphoreType.DMA((nb,)),
        ],
        compiler_params=params(60),
        cost_estimate=cost(4 * ROWS * (nb * ROWS + TEXT) * W, 8 * 2**20, ROWS * nb * ROWS * NH),
        name="early",
    )(wm, tlen, q, every, *blocks)


def late_kernel(wm, q_ref, b0, b1, b2, acc_ref, m_ref, l_ref, *rest):
    o_ref = rest[-1]
    blocks = (b0, b1, b2)
    fcol = 2 * lax.rem(lax.axis_index("tile"), 2)
    rowof = (1, 0, 2)
    for t in range(2):
        rs = pl.ds(t * TT, TT)
        parts = []
        mx = None
        for b in range(3):
            s = scores(q_ref[rs, :], blocks[b][:ROWS, :])
            for f in range(2):
                sf = s[:, f * TT : (f + 1) * TT] * SCALE + bias_of(wm, t, f, rowof[b], fcol)
                parts.append(sf)
                fx = fold(sf, jnp.maximum)
                mx = fx if mx is None else jnp.maximum(mx, fx)
        mo = m_ref[rs, :]
        mn = jnp.maximum(mo, spread(jnp.max(mx, axis=1, keepdims=True)))
        al = jnp.exp2(mo - mn)
        acc = acc_ref[rs, :] * al
        tot = l_ref[rs, :] * al
        for b in range(3):
            p = jnp.concatenate(
                [
                    jnp.exp2(parts[2 * b + f][:, i * HD : (i + 1) * HD] - mn)
                    for f in range(2)
                    for i in range(2)
                ],
                axis=1,
            )
            tot += fold(p, jnp.add)
            acc += jnp.dot(p.astype(BF16), blocks[b][ROWS:, :], preferred_element_type=F32)
        o = (acc / jnp.sum(tot, axis=1, keepdims=True)).astype(BF16)
        for x in range(4):
            o_ref[x, rs, :] = o


def late(wm, q, far, acc, m, l, *deps):
    head = pl.BlockSpec((ROWS, HD), lambda i: (0, i))
    block = pl.BlockSpec((2 * ROWS, HD), lambda i: (0, i))
    return pl.pallas_call(
        late_kernel,
        grid=(NH,),
        out_shape=jax.ShapeDtypeStruct((4, ROWS, W), BF16),
        in_specs=[SM, head, block, block, block, head, head, head] + [ANY] * len(deps),
        out_specs=pl.BlockSpec((4, ROWS, HD), lambda i: (0, 0, i)),
        compiler_params=params(60),
        cost_estimate=cost(12 * ROWS * ROWS * W, 2 * 2**20, 3 * ROWS * ROWS),
        name="late",
    )(wm, q, *far, acc, m, l, *deps)


def columns(xd, j):
    z = lax.axis_index("head") // 4
    return pl.ds(pl.multiple_of(((z + j - 2 * j * z) * 4 + xd) * W, HD), W)


def pieces3(x):
    hi = x.astype(BF16).astype(F32)
    mid = (x - hi).astype(BF16).astype(F32)
    return hi, mid, x - hi - mid


def text_kernel(t_ref, kv_ref, *rest):
    msg_ref = rest[-1]
    lane = lax.broadcasted_iota(jnp.int32, (TEXT, HD), 1)
    stat = jnp.zeros((TEXT, HD), F32)
    for h in range(NH):
        hs = pl.ds(h * HD, HD)
        s = scores(t_ref[:, hs], kv_ref[:ROWS, hs]) * SCALE
        m = jnp.max(fold(s, jnp.maximum), axis=1, keepdims=True)
        p = jnp.exp2(s - m)
        tot = jnp.sum(fold(p, jnp.add), axis=1, keepdims=True)
        acc = jnp.dot(p.astype(BF16), kv_ref[ROWS:, hs], preferred_element_type=F32)
        msg_ref[:, hs] = (acc / tot).astype(BF16)
        for j, piece in enumerate(pieces3(m + jnp.log2(tot))):
            stat = jnp.where(lane == 8 * j + h, spread(piece), stat)
    msg_ref[:, W:] = stat.astype(BF16)


def text_part(every, kv, *deps):
    return pl.pallas_call(
        text_kernel,
        out_shape=jax.ShapeDtypeStruct((TEXT, W + HD), BF16),
        in_specs=[VM, VM] + [ANY] * len(deps),
        out_specs=VM,
        compiler_params=params(60),
        cost_estimate=cost(4 * TEXT * ROWS * W, 2 * 2**20, TEXT * ROWS * NH),
        name="text_part",
    )(every, kv, *deps)


def merge_kernel(tlen, msg_ref, tq_ref, t_ref, proj_ref, o0, o1, o2, o3, flat):
    msg = msg_ref[...].astype(F32)
    stat = msg[:, W:]
    slane = lax.broadcasted_iota(jnp.int32, (TEXT, HD), 1)
    lane = lax.broadcasted_iota(jnp.int32, (1, TEXT), 1)
    tbias = jnp.where(lane < tlen[0], 0.0, -BIG)
    q = tq_ref[...]
    attn = []
    for h in range(NH):
        hs = slice(h * HD, (h + 1) * HD)
        s = scores(q[:, hs], t_ref[:, pl.ds(W + h * HD, HD)]) * SCALE + tbias
        m = jnp.max(s, axis=1, keepdims=True)
        p = jnp.exp2(s - m)
        tot = jnp.sum(p, axis=1, keepdims=True)
        own = jnp.dot(p.astype(BF16), t_ref[:, pl.ds(2 * W + h * HD, HD)], preferred_element_type=F32)
        mine = (slane == h) | (slane == 8 + h) | (slane == 16 + h)
        lse = jnp.sum(jnp.where(mine, stat, 0.0), axis=1, keepdims=True)
        lse = spread(lse).reshape(TEXT // TL, TL, HD)
        peak = jnp.maximum(jnp.max(lse, axis=0), spread(m))
        wt = jnp.exp2(lse - peak[None])
        w0 = jnp.exp2(spread(m) - peak)
        num = jnp.sum(wt * msg[:, hs].reshape(TEXT // TL, TL, HD), axis=0) + w0 * own
        den = jnp.sum(wt, axis=0) + w0 * tot
        attn.append((num / den).astype(BF16))
    a = jnp.concatenate(attn, axis=1)
    flat[...] = jnp.dot(a, proj_ref[...], preferred_element_type=F32)
    x = lax.rem(lax.axis_index("head"), 4)
    for d, out in enumerate((o0, o1, o2, o3)):
        for j in range(2):
            cs = columns(lax.rem(x + d, 4), j)
            out[:, j * W : (j + 1) * W] = flat[:, cs].astype(BF16)


def text_merge(tlen, msg, tq, every, proj):
    return pl.pallas_call(
        merge_kernel,
        out_shape=(jax.ShapeDtypeStruct((TL, 2 * W), BF16),) * 4,
        in_specs=[SM, VM, VM, VM, VM],
        out_specs=(VM,) * 4,
        scratch_shapes=[pltpu.VMEM((TL, 8 * W), F32)],
        compiler_params=params(60),
        cost_estimate=cost(2 * TL * W * 8 * W, 3 * 2**20, TEXT * HD * NH),
        name="text_merge",
    )(tlen, msg, tq, every, proj)


def split_kernel(proj_ref, *rest):
    x = lax.rem(lax.axis_index("head"), 4)
    for d, out in enumerate(rest[-4:]):
        for j in range(2):
            out[:, j * W : (j + 1) * W] = proj_ref[:, columns(lax.rem(x + d, 4), j)]


def split_proj(proj, *deps):
    return pl.pallas_call(
        split_kernel,
        out_shape=(jax.ShapeDtypeStruct((W, 2 * W), BF16),) * 4,
        in_specs=[VM] + [ANY] * len(deps),
        out_specs=(VM,) * 4,
        compiler_params=params(60),
        cost_estimate=cost(0, 5 * 2**20),
        name="split_proj",
    )(proj, *deps)


def pack_kernel(k_ref, v_ref, tq_ref, tk_ref, tv_ref, kv_ref, t_ref, buf, sem):
    copies = [
        pltpu.make_async_copy(r, d, sem.at[i])
        for i, (r, d) in enumerate(
            (
                (k_ref, kv_ref.at[pl.ds(0, ROWS)]),
                (v_ref, kv_ref.at[pl.ds(ROWS, ROWS)]),
                (tq_ref, buf.at[0]),
                (tk_ref, buf.at[1]),
                (tv_ref, buf.at[2]),
            )
        )
    ]
    for c in copies:
        c.start()
    for c in copies[2:]:
        c.wait()
    both = jnp.concatenate([buf[i] for i in range(3)], axis=1)
    for i in range(32):
        t_ref[i] = both
    for c in copies[:2]:
        c.wait()


def pack(k, v, tq, tk, tv):
    return pl.pallas_call(
        pack_kernel,
        out_shape=(
            jax.ShapeDtypeStruct((2 * ROWS, W), BF16),
            jax.ShapeDtypeStruct((32, TL, 3 * W), BF16),
        ),
        in_specs=[HBM] * 5,
        out_specs=(VM, VM),
        scratch_shapes=[pltpu.VMEM((3, TL, W), BF16), pltpu.SemaphoreType.DMA((5,))],
        compiler_params=params(60),
        cost_estimate=cost(0, 2 * 2**20),
        name="pack",
    )(k, v, tq, tk, tv)


def after_kernel(x_ref, *rest):
    pass


def after(x, *deps):
    return pl.pallas_call(
        after_kernel,
        out_shape=jax.ShapeDtypeStruct(x.shape, x.dtype),
        in_specs=[ANY] * (1 + len(deps)),
        out_specs=ANY,
        input_output_aliases={0: 0},
        compiler_params=params(60),
        cost_estimate=cost(0, 1),
        name="after",
    )(x, *deps)


def project_kernel(
    a_ref, w0, w1, w2, w3, t0, t1, t2, t3, own_ref, away_ref, abuf, wbuf, acc, sem
):
    me = lax.rem(lax.axis_index("head"), 4)
    copies = []
    for x, w_ref in enumerate((w0, w1, w2, w3)):
        a_at = a_ref.at[lax.rem(me + 4 - x, 4)]
        for i, (src, dst) in enumerate(((w_ref, wbuf), (a_at, abuf))):
            copies.append(pltpu.make_async_copy(src, dst.at[x], sem.at[2 * x + i]))
            copies[-1].start()
    t = sum(r[...].astype(F32) for r in (t0, t1, t2, t3))
    t = jnp.concatenate([t, jnp.zeros_like(t)], axis=0)
    own_ref[pl.ds(ROWS, 16), :] = t[:, :W]
    away_ref[pl.ds(ROWS, 16), :] = t[:, W:].astype(BF16)
    for x in range(4):
        for c in copies[2 * x : 2 * x + 2]:
            c.wait()
        o = jnp.dot(abuf[x], wbuf[x], preferred_element_type=F32)
        if x > 0:
            o += acc[...]
        if x < 3:
            acc[...] = o
        else:
            own_ref[:ROWS, :] = o[:, :W]
            away_ref[:ROWS, :] = o[:, W:].astype(BF16)


def project(attn, proj, text):
    return pl.pallas_call(
        project_kernel,
        out_shape=(
            jax.ShapeDtypeStruct((ROWS + 16, W), F32),
            jax.ShapeDtypeStruct((ROWS + 16, W), BF16),
        ),
        in_specs=[ANY] * 5 + [VM] * 4,
        out_specs=(VM, VM),
        scratch_shapes=[
            pltpu.VMEM((4, ROWS, W), BF16),
            pltpu.VMEM((4, W, 2 * W), BF16),
            pltpu.VMEM((ROWS, 2 * W), F32),
            pltpu.SemaphoreType.DMA((8,)),
        ],
        compiler_params=params(24),
        cost_estimate=cost(2 * ROWS * 4 * W * 2 * W, 6 * 2**20),
        name="project",
    )(attn, *proj, *text)


def add_kernel(own_ref, got_ref, video_ref, text_ref):
    video_ref[...] = (own_ref[:ROWS, :] + got_ref[:ROWS, :].astype(F32)).astype(BF16)
    t = own_ref[pl.ds(ROWS, 16), :] + got_ref[pl.ds(ROWS, 16), :].astype(F32)
    text_ref[...] = t[:TL, :].astype(BF16)


def add_up(own, got):
    return pl.pallas_call(
        add_kernel,
        out_shape=(jax.ShapeDtypeStruct((ROWS, W), BF16), jax.ShapeDtypeStruct((TL, W), BF16)),
        in_specs=[VM, VM],
        out_specs=(VM, VM),
        compiler_params=params(8),
        cost_estimate=cost(0, 2 * 2**20),
        name="add_up",
    )(own, got)


def per_device(
    video_q, video_k, video_v, text_q, text_k, text_v, video_proj, text_proj, window_mask, text_length
):
    kv, text = pack(video_k, video_v, text_q, text_k, text_v)
    far = over_chip(kv)
    up = rows_on(kv, 1)
    dn = rows_on(kv, -1)
    side = other_core(kv)

    proj = split_proj(video_proj)
    proj = [x_on(p, d) if d else p for d, p in enumerate(proj)]
    every = lax.all_to_all(text, "tile", 0, 0, tiled=True).reshape(TEXT, 3 * W)
    far_up, far_dn = rows_on(far, 1), rows_on(far, -1)
    up, dn = after(up, every, proj[0]), after(dn, every, proj[0])
    side_up, side_dn = other_core(up), other_core(dn)
    acc, m, l = early(
        window_mask, text_length, video_q, every, (kv, up, dn, side, side_up, side_dn)
    )
    msg = text_part(every, kv).reshape(32, TL, W + HD)
    msg = after(msg, far_up, far_dn, acc)
    got = lax.all_to_all(msg, "tile", 0, 0, tiled=True).reshape(TEXT, W + HD)

    attn = x_swap(late(window_mask, video_q, (far, far_up, far_dn), acc, m, l, *proj[1:]))
    parts = text_merge(text_length, got, text_q, every, text_proj)
    parts = [x_on(p, d) if d else p for d, p in enumerate(parts)]
    own, away = project(attn, proj, parts)
    return add_up(own, z_pair(away))


def solution(mesh):
    both, rows = P("tile", "head"), P("head", None)
    return jax.shard_map(
        per_device,
        mesh=mesh,
        in_specs=(both,) * 6 + (rows, rows, P("tile", None), P()),
        out_specs=(both, both),
        check_vma=False,
    )
```

```python
import functools
import math

import jax
import jax.numpy as jnp
from jax import lax
from jax.experimental import pallas as pl
from jax.experimental.pallas import tpu as pltpu
from jax.sharding import PartitionSpec as P

HD = 128
TT = 256
NH = 3
W = NH * HD
TEXT = 256
TL = 8
ROWS = 2 * TT
SCALE = math.log2(math.e) / math.sqrt(HD)
HALF = W // 2
BIG = 1e30
F32 = jnp.float32
BF16 = jnp.bfloat16

ANY = pl.BlockSpec(memory_space=pl.ANY)
SM = pl.BlockSpec(memory_space=pltpu.SMEM)
VM = pl.BlockSpec(memory_space=pltpu.VMEM)
HBM = pl.BlockSpec(memory_space=pltpu.HBM)


def params(mib):
    return pltpu.CompilerParams(vmem_limit_bytes=mib * 2**20)


def cost(flops, nbytes, exps=0):
    return pl.CostEstimate(flops=1, bytes_accessed=1, transcendentals=1)


def rows_on(x, d):
    return lax.ppermute(x, "tile", [(i, ((i // 8 + d) % 4) * 8 + i % 8) for i in range(32)])


def over_chip(x):
    return lax.ppermute(
        x, "tile", [(i, (i // 8) * 8 + (i % 8 + (1 if i % 2 else -1)) % 8) for i in range(32)]
    )


def other_core(x):
    return lax.ppermute(x, "tile", [(i, i ^ 1) for i in range(32)])


def x_swap(x):
    groups = [[0, 1, 2, 3], [4, 5, 6, 7]]
    return lax.all_to_all(x, "head", 0, 0, tiled=True, axis_index_groups=groups)


def x_on(x, d):
    return lax.ppermute(x, "head", [(i, (i // 4) * 4 + (i + d) % 4) for i in range(8)])


def z_pair(x):
    return lax.ppermute(x, "head", [(i, i ^ 4) for i in range(8)])


def fold(x, op):
    r = x[:, :HD]
    for i in range(1, x.shape[1] // HD):
        r = op(r, x[:, i * HD : (i + 1) * HD])
    return r


def scores(q, k):
    return lax.dot_general(q, k, (((1,), (1,)), ((), ())), preferred_element_type=F32)


def spread(col):
    return jnp.broadcast_to(col, (col.shape[0], HD))


def bias_of(wm, tile, frame, row, col):
    live = wm[tile, 9 * (frame - tile + 1) + 3 * row + col]
    return jnp.where(live > 0, 0.0, -BIG).astype(F32)


def early_kernel(
    wm, tlen, q_ref, t_ref, b0, b1, b2, b3, b4, b5, acc_ref, m_ref, l_ref, kbuf, s_s, mx_s, sem
):
    blocks = (b0, b1, b2, b3, b4, b5)
    nb = len(blocks)
    for b in range(nb):
        pltpu.make_async_copy(blocks[b], kbuf.at[b], sem.at[b]).start()
    lane = lax.broadcasted_iota(jnp.int32, (1, TEXT), 1)
    tbias = jnp.where(lane < tlen[0], 0.0, -BIG)
    pcol = 2 - 2 * lax.rem(lax.axis_index("tile"), 2)
    colof = (1, 1, 1, pcol, pcol, pcol)
    rowof = (1, 0, 2, 1, 0, 2)

    def hs(h):
        return pl.ds(h * HD, HD)

    def p1_text(h, w):
        for t in range(2):
            k = t_ref[:, pl.ds(W + h * HD, HD)]
            s = scores(q_ref[pl.ds(t * TT, TT), hs(h)], k) * SCALE + tbias
            s_s[w, t, nb, :, :TEXT] = s
            mx_s[w, t] = fold(s, jnp.maximum)

    def p1(h, w, b):
        k = kbuf[b, :ROWS, hs(h)]
        for t in range(2):
            s = scores(q_ref[pl.ds(t * TT, TT), hs(h)], k)
            mx = mx_s[w, t]
            for f in range(2):
                sf = s[:, f * TT : (f + 1) * TT] * SCALE + bias_of(wm, t, f, rowof[b], colof[b])
                s_s[w, t, b, :, f * TT : (f + 1) * TT] = sf
                mx = jnp.maximum(mx, fold(sf, jnp.maximum))
            mx_s[w, t] = mx

    def top(h, w):
        for t in range(2):
            m_ref[pl.ds(t * TT, TT), hs(h)] = spread(jnp.max(mx_s[w, t], axis=1, keepdims=True))

    def weigh(s, m):
        return jnp.concatenate(
            [jnp.exp2(s[:, i * HD : (i + 1) * HD] - m) for i in range(s.shape[1] // HD)], axis=1
        )

    def p2_text(h, w):
        for t in range(2):
            rs = pl.ds(t * TT, TT)
            p = weigh(s_s[w, t, nb, :, :TEXT], m_ref[rs, hs(h)])
            l_ref[rs, hs(h)] = fold(p, jnp.add)
            v = t_ref[:, pl.ds(2 * W + h * HD, HD)]
            acc_ref[rs, hs(h)] = jnp.dot(p.astype(BF16), v, preferred_element_type=F32)

    def p2(h, w, b):
        v = kbuf[b, ROWS:, hs(h)]
        for t in range(2):
            rs = pl.ds(t * TT, TT)
            p = weigh(s_s[w, t, b], m_ref[rs, hs(h)])
            l_ref[rs, hs(h)] += fold(p, jnp.add)
            acc_ref[rs, hs(h)] += jnp.dot(p.astype(BF16), v, preferred_element_type=F32)

    p1_text(0, 0)
    for b in range(nb):
        pltpu.make_async_copy(blocks[b], kbuf.at[b], sem.at[b]).wait()
        p1(0, 0, b)
    top(0, 0)
    for h in range(NH):
        w = h % 2
        p2_text(h, w)
        if h + 1 < NH:
            p1_text(h + 1, 1 - w)
        for b in range(nb):
            p2(h, w, b)
            if h + 1 < NH:
                p1(h + 1, 1 - w, b)
        if h + 1 < NH:
            top(h + 1, 1 - w)


def early(wm, tlen, q, every, blocks):
    nb = len(blocks)
    part = jax.ShapeDtypeStruct((ROWS, W), F32)
    return pl.pallas_call(
        early_kernel,
        out_shape=(part, part, part),
        in_specs=[SM, SM, VM, VM] + [ANY] * nb,
        out_specs=(VM, VM, VM),
        scratch_shapes=[
            pltpu.VMEM((nb, 2 * ROWS, W), BF16),
            pltpu.VMEM((2, 2, nb + 1, TT, ROWS), F32),
            pltpu.VMEM((2, 2, TT, HD), F32),
            pltpu.SemaphoreType.DMA((nb,)),
        ],
        compiler_params=params(60),
        cost_estimate=cost(4 * ROWS * (nb * ROWS + TEXT) * W, 8 * 2**20, ROWS * nb * ROWS * NH),
        name="early",
    )(wm, tlen, q, every, *blocks)


def late_kernel(wm, q_ref, b0, b1, b2, acc_ref, m_ref, l_ref, *rest):
    o_ref = rest[-1]
    blocks = (b0, b1, b2)
    fcol = 2 * lax.rem(lax.axis_index("tile"), 2)
    rowof = (1, 0, 2)
    for t in range(2):
        rs = pl.ds(t * TT, TT)
        parts = []
        mx = None
        for b in range(3):
            s = scores(q_ref[rs, :], blocks[b][:ROWS, :])
            for f in range(2):
                sf = s[:, f * TT : (f + 1) * TT] * SCALE + bias_of(wm, t, f, rowof[b], fcol)
                parts.append(sf)
                fx = fold(sf, jnp.maximum)
                mx = fx if mx is None else jnp.maximum(mx, fx)
        mo = m_ref[rs, :]
        mn = jnp.maximum(mo, spread(jnp.max(mx, axis=1, keepdims=True)))
        al = jnp.exp2(mo - mn)
        acc = acc_ref[rs, :] * al
        tot = l_ref[rs, :] * al
        for b in range(3):
            p = jnp.concatenate(
                [
                    jnp.exp2(parts[2 * b + f][:, i * HD : (i + 1) * HD] - mn)
                    for f in range(2)
                    for i in range(2)
                ],
                axis=1,
            )
            tot += fold(p, jnp.add)
            acc += jnp.dot(p.astype(BF16), blocks[b][ROWS:, :], preferred_element_type=F32)
        o = (acc / jnp.sum(tot, axis=1, keepdims=True)).astype(BF16)
        for x in range(4):
            o_ref[x, rs, :] = o


def late(wm, q, far, acc, m, l, *deps):
    head = pl.BlockSpec((ROWS, HD), lambda i: (0, i))
    block = pl.BlockSpec((2 * ROWS, HD), lambda i: (0, i))
    return pl.pallas_call(
        late_kernel,
        grid=(NH,),
        out_shape=jax.ShapeDtypeStruct((4, ROWS, W), BF16),
        in_specs=[SM, head, block, block, block, head, head, head] + [ANY] * len(deps),
        out_specs=pl.BlockSpec((4, ROWS, HD), lambda i: (0, 0, i)),
        compiler_params=params(60),
        cost_estimate=cost(12 * ROWS * ROWS * W, 2 * 2**20, 3 * ROWS * ROWS),
        name="late",
    )(wm, q, *far, acc, m, l, *deps)


def columns(xd, j):
    z = lax.axis_index("head") // 4
    return pl.ds(pl.multiple_of(((z + j - 2 * j * z) * 4 + xd) * W, HD), W)


def pieces3(x):
    hi = x.astype(BF16).astype(F32)
    mid = (x - hi).astype(BF16).astype(F32)
    return hi, mid, x - hi - mid


def text_kernel(t_ref, kv_ref, *rest):
    msg_ref = rest[-1]
    lane = lax.broadcasted_iota(jnp.int32, (TEXT, HD), 1)
    stat = jnp.zeros((TEXT, HD), F32)
    for h in range(NH):
        hs = pl.ds(h * HD, HD)
        s = scores(t_ref[:, hs], kv_ref[:ROWS, hs]) * SCALE
        m = jnp.max(fold(s, jnp.maximum), axis=1, keepdims=True)
        p = jnp.exp2(s - m)
        tot = jnp.sum(fold(p, jnp.add), axis=1, keepdims=True)
        acc = jnp.dot(p.astype(BF16), kv_ref[ROWS:, hs], preferred_element_type=F32)
        msg_ref[:, hs] = (acc / tot).astype(BF16)
        for j, piece in enumerate(pieces3(m + jnp.log2(tot))):
            stat = jnp.where(lane == 8 * j + h, spread(piece), stat)
    msg_ref[:, W:] = stat.astype(BF16)


def text_part(every, kv, *deps):
    return pl.pallas_call(
        text_kernel,
        out_shape=jax.ShapeDtypeStruct((TEXT, W + HD), BF16),
        in_specs=[VM, VM] + [ANY] * len(deps),
        out_specs=VM,
        compiler_params=params(60),
        cost_estimate=cost(4 * TEXT * ROWS * W, 2 * 2**20, TEXT * ROWS * NH),
        name="text_part",
    )(every, kv, *deps)


def merge_kernel(tlen, msg_ref, tq_ref, t_ref, proj_ref, o0, o1, o2, o3, flat):
    msg = msg_ref[...].astype(F32)
    stat = msg[:, W:]
    slane = lax.broadcasted_iota(jnp.int32, (TEXT, HD), 1)
    lane = lax.broadcasted_iota(jnp.int32, (1, TEXT), 1)
    tbias = jnp.where(lane < tlen[0], 0.0, -BIG)
    q = tq_ref[...]
    attn = []
    for h in range(NH):
        hs = slice(h * HD, (h + 1) * HD)
        s = scores(q[:, hs], t_ref[:, pl.ds(W + h * HD, HD)]) * SCALE + tbias
        m = jnp.max(s, axis=1, keepdims=True)
        p = jnp.exp2(s - m)
        tot = jnp.sum(p, axis=1, keepdims=True)
        own = jnp.dot(p.astype(BF16), t_ref[:, pl.ds(2 * W + h * HD, HD)], preferred_element_type=F32)
        mine = (slane == h) | (slane == 8 + h) | (slane == 16 + h)
        lse = jnp.sum(jnp.where(mine, stat, 0.0), axis=1, keepdims=True)
        lse = spread(lse).reshape(TEXT // TL, TL, HD)
        peak = jnp.maximum(jnp.max(lse, axis=0), spread(m))
        wt = jnp.exp2(lse - peak[None])
        w0 = jnp.exp2(spread(m) - peak)
        num = jnp.sum(wt * msg[:, hs].reshape(TEXT // TL, TL, HD), axis=0) + w0 * own
        den = jnp.sum(wt, axis=0) + w0 * tot
        attn.append((num / den).astype(BF16))
    a = jnp.concatenate(attn, axis=1)
    flat[...] = jnp.dot(a, proj_ref[...], preferred_element_type=F32)
    x = lax.rem(lax.axis_index("head"), 4)
    for d, out in enumerate((o0, o1, o2, o3)):
        for j in range(2):
            cs = columns(lax.rem(x + d, 4), j)
            out[:, j * W : (j + 1) * W] = flat[:, cs].astype(BF16)


def text_merge(tlen, msg, tq, every, proj):
    return pl.pallas_call(
        merge_kernel,
        out_shape=(jax.ShapeDtypeStruct((TL, 2 * W), BF16),) * 4,
        in_specs=[SM, VM, VM, VM, VM],
        out_specs=(VM,) * 4,
        scratch_shapes=[pltpu.VMEM((TL, 8 * W), F32)],
        compiler_params=params(60),
        cost_estimate=cost(2 * TL * W * 8 * W, 3 * 2**20, TEXT * HD * NH),
        name="text_merge",
    )(tlen, msg, tq, every, proj)


def split_kernel(proj_ref, after_ref, out_ref):
    core = lax.rem(lax.axis_index("tile"), 2)
    mine = pl.ds(pl.multiple_of(core * HALF, 16), HALF)
    for xd in range(4):
        for j in range(2):
            out_ref[xd, :, j * W : (j + 1) * W] = proj_ref[mine, columns(xd, j)]


def split_proj(proj, after_this):
    return pl.pallas_call(
        split_kernel,
        out_shape=jax.ShapeDtypeStruct((4, HALF, 2 * W), BF16),
        in_specs=[VM, ANY],
        out_specs=VM,
        compiler_params=params(60),
        cost_estimate=cost(0, 5 * 2**20),
        name="split_proj",
    )(proj, after_this)


def pack_kernel(k_ref, v_ref, tq_ref, tk_ref, tv_ref, kv_ref, t_ref, buf, sem):
    copies = [
        pltpu.make_async_copy(r, d, sem.at[i])
        for i, (r, d) in enumerate(
            (
                (k_ref, kv_ref.at[pl.ds(0, ROWS)]),
                (v_ref, kv_ref.at[pl.ds(ROWS, ROWS)]),
                (tq_ref, buf.at[0]),
                (tk_ref, buf.at[1]),
                (tv_ref, buf.at[2]),
            )
        )
    ]
    for c in copies:
        c.start()
    for c in copies[2:]:
        c.wait()
    both = jnp.concatenate([buf[i] for i in range(3)], axis=1)
    for i in range(32):
        t_ref[i] = both
    for c in copies[:2]:
        c.wait()


def pack(k, v, tq, tk, tv):
    return pl.pallas_call(
        pack_kernel,
        out_shape=(
            jax.ShapeDtypeStruct((2 * ROWS, W), BF16),
            jax.ShapeDtypeStruct((32, TL, 3 * W), BF16),
        ),
        in_specs=[HBM] * 5,
        out_specs=(VM, VM),
        scratch_shapes=[pltpu.VMEM((3, TL, W), BF16), pltpu.SemaphoreType.DMA((5,))],
        compiler_params=params(60),
        cost_estimate=cost(0, 2 * 2**20),
        name="pack",
    )(k, v, tq, tk, tv)


def after_kernel(x_ref, *rest):
    pass


def after(x, *deps):
    return pl.pallas_call(
        after_kernel,
        out_shape=jax.ShapeDtypeStruct(x.shape, x.dtype),
        in_specs=[ANY] * (1 + len(deps)),
        out_specs=ANY,
        input_output_aliases={0: 0},
        compiler_params=params(60),
        cost_estimate=cost(0, 1),
        name="after",
    )(x, *deps)


def project_kernel(
    a_ref, w_ref, v_ref, t0, t1, t2, t3, own_ref, away_ref, abuf, wbuf, acc, sem
):
    core = lax.rem(lax.axis_index("tile"), 2)
    copies = []
    for x in range(4):
        for i, (src, dst) in enumerate(
            (
                (w_ref, wbuf.at[x, pl.ds(pl.multiple_of(core * HALF, 16), HALF)]),
                (v_ref, wbuf.at[x, pl.ds(pl.multiple_of((1 - core) * HALF, 16), HALF)]),
                (a_ref, abuf.at[x]),
            )
        ):
            copies.append(pltpu.make_async_copy(src.at[x], dst, sem.at[3 * x + i]))
            copies[-1].start()
    t = sum(r[...].astype(F32) for r in (t0, t1, t2, t3))
    t = jnp.concatenate([t, jnp.zeros_like(t)], axis=0)
    own_ref[pl.ds(ROWS, 16), :] = t[:, :W]
    away_ref[pl.ds(ROWS, 16), :] = t[:, W:].astype(BF16)
    for x in range(4):
        for c in copies[3 * x : 3 * x + 3]:
            c.wait()
        o = jnp.dot(abuf[x], wbuf[x], preferred_element_type=F32)
        if x > 0:
            o += acc[...]
        if x < 3:
            acc[...] = o
        else:
            own_ref[:ROWS, :] = o[:, :W]
            away_ref[:ROWS, :] = o[:, W:].astype(BF16)


def project(attn, proj, text):
    return pl.pallas_call(
        project_kernel,
        out_shape=(
            jax.ShapeDtypeStruct((ROWS + 16, W), F32),
            jax.ShapeDtypeStruct((ROWS + 16, W), BF16),
        ),
        in_specs=[ANY] * 3 + [VM] * 4,
        out_specs=(VM, VM),
        scratch_shapes=[
            pltpu.VMEM((4, ROWS, W), BF16),
            pltpu.VMEM((4, W, 2 * W), BF16),
            pltpu.VMEM((ROWS, 2 * W), F32),
            pltpu.SemaphoreType.DMA((12,)),
        ],
        compiler_params=params(24),
        cost_estimate=cost(2 * ROWS * 4 * W * 2 * W, 6 * 2**20),
        name="project",
    )(attn, *proj, *text)


def add_kernel(own_ref, got_ref, video_ref, text_ref):
    video_ref[...] = (own_ref[:ROWS, :] + got_ref[:ROWS, :].astype(F32)).astype(BF16)
    t = own_ref[pl.ds(ROWS, 16), :] + got_ref[pl.ds(ROWS, 16), :].astype(F32)
    text_ref[...] = t[:TL, :].astype(BF16)


def add_up(own, got):
    return pl.pallas_call(
        add_kernel,
        out_shape=(jax.ShapeDtypeStruct((ROWS, W), BF16), jax.ShapeDtypeStruct((TL, W), BF16)),
        in_specs=[VM, VM],
        out_specs=(VM, VM),
        compiler_params=params(8),
        cost_estimate=cost(0, 2 * 2**20),
        name="add_up",
    )(own, got)


def per_device(
    video_q, video_k, video_v, text_q, text_k, text_v, video_proj, text_proj, window_mask, text_length
):
    kv, text = pack(video_k, video_v, text_q, text_k, text_v)
    far = over_chip(kv)
    up = rows_on(kv, 1)
    dn = rows_on(kv, -1)
    side = other_core(kv)

    every = lax.all_to_all(text, "tile", 0, 0, tiled=True).reshape(TEXT, 3 * W)
    far_up, far_dn = rows_on(far, 1), rows_on(far, -1)
    msg = text_part(every, kv)
    pieces = split_proj(video_proj, msg)
    proj = x_swap(pieces)
    up, dn = after(up, msg, pieces), after(dn, msg, pieces)
    side_up, side_dn = other_core(up), other_core(dn)
    acc, m, l = early(
        window_mask, text_length, video_q, every, (kv, up, dn, side, side_up, side_dn)
    )
    msg = after(msg.reshape(32, TL, W + HD), acc)
    got = lax.all_to_all(msg, "tile", 0, 0, tiled=True).reshape(TEXT, W + HD)

    attn = x_swap(late(window_mask, video_q, (far, far_up, far_dn), acc, m, l))
    parts = text_merge(text_length, got, text_q, every, text_proj)
    parts = [x_on(p, d) if d else p for d, p in enumerate(parts)]
    own, away = project(attn, (proj, other_core(proj)), parts)
    return add_up(own, z_pair(away))


def solution(mesh):
    both, rows = P("tile", "head"), P("head", None)
    return jax.shard_map(
        per_device,
        mesh=mesh,
        in_specs=(both,) * 6 + (rows, rows, P("tile", None), P()),
        out_specs=(both, both),
        check_vma=False,
    )
```

```python
import functools
import math

import jax
import jax.numpy as jnp
from jax import lax
from jax.experimental import pallas as pl
from jax.experimental.pallas import tpu as pltpu
from jax.sharding import PartitionSpec as P

HD = 128
TT = 256
NH = 3
W = NH * HD
TEXT = 256
TL = 8
ROWS = 2 * TT
SCALE = math.log2(math.e) / math.sqrt(HD)
HALF = W // 2
BIG = 1e30
F32 = jnp.float32
BF16 = jnp.bfloat16

ANY = pl.BlockSpec(memory_space=pl.ANY)
SM = pl.BlockSpec(memory_space=pltpu.SMEM)
VM = pl.BlockSpec(memory_space=pltpu.VMEM)
HBM = pl.BlockSpec(memory_space=pltpu.HBM)


def params(mib):
    return pltpu.CompilerParams(vmem_limit_bytes=mib * 2**20)


def cost(flops, nbytes, exps=0):
    return pl.CostEstimate(flops=1, bytes_accessed=1, transcendentals=1)


def rows_on(x, d):
    return lax.ppermute(x, "tile", [(i, ((i // 8 + d) % 4) * 8 + i % 8) for i in range(32)])


def over_chip(x):
    return lax.ppermute(
        x, "tile", [(i, (i // 8) * 8 + (i % 8 + (1 if i % 2 else -1)) % 8) for i in range(32)]
    )


def other_core(x):
    return lax.ppermute(x, "tile", [(i, i ^ 1) for i in range(32)])


def x_swap(x):
    groups = [[0, 1, 2, 3], [4, 5, 6, 7]]
    return lax.all_to_all(x, "head", 0, 0, tiled=True, axis_index_groups=groups)


def x_on(x, d):
    return lax.ppermute(x, "head", [(i, (i // 4) * 4 + (i + d) % 4) for i in range(8)])


def z_pair(x):
    return lax.ppermute(x, "head", [(i, i ^ 4) for i in range(8)])


def fold(x, op):
    r = x[:, :HD]
    for i in range(1, x.shape[1] // HD):
        r = op(r, x[:, i * HD : (i + 1) * HD])
    return r


def scores(q, k):
    return lax.dot_general(q, k, (((1,), (1,)), ((), ())), preferred_element_type=F32)


def spread(col):
    return jnp.broadcast_to(col, (col.shape[0], HD))


def bias_of(wm, tile, frame, row, col):
    live = wm[tile, 9 * (frame - tile + 1) + 3 * row + col]
    return jnp.where(live > 0, 0.0, -BIG).astype(F32)


def early_kernel(
    wm, tlen, q_ref, t_ref, b0, b1, b2, b3, b4, b5, acc_ref, m_ref, l_ref, kbuf, s_s, mx_s, sem
):
    blocks = (b0, b1, b2, b3, b4, b5)
    nb = len(blocks)
    for b in range(nb):
        pltpu.make_async_copy(blocks[b], kbuf.at[b], sem.at[b]).start()
    lane = lax.broadcasted_iota(jnp.int32, (1, TEXT), 1)
    tbias = jnp.where(lane < tlen[0], 0.0, -BIG)
    pcol = 2 - 2 * lax.rem(lax.axis_index("tile"), 2)
    colof = (1, 1, 1, pcol, pcol, pcol)
    rowof = (1, 0, 2, 1, 0, 2)

    def hs(h):
        return pl.ds(h * HD, HD)

    def p1_text(h, w):
        for t in range(2):
            k = t_ref[:, pl.ds(W + h * HD, HD)]
            s = scores(q_ref[pl.ds(t * TT, TT), hs(h)], k) * SCALE + tbias
            s_s[w, t, nb, :, :TEXT] = s
            mx_s[w, t] = fold(s, jnp.maximum)

    def p1(h, w, b):
        k = kbuf[b, :ROWS, hs(h)]
        for t in range(2):
            s = scores(q_ref[pl.ds(t * TT, TT), hs(h)], k)
            mx = mx_s[w, t]
            for f in range(2):
                sf = s[:, f * TT : (f + 1) * TT] * SCALE + bias_of(wm, t, f, rowof[b], colof[b])
                s_s[w, t, b, :, f * TT : (f + 1) * TT] = sf
                mx = jnp.maximum(mx, fold(sf, jnp.maximum))
            mx_s[w, t] = mx

    def top(h, w):
        for t in range(2):
            m_ref[pl.ds(t * TT, TT), hs(h)] = spread(jnp.max(mx_s[w, t], axis=1, keepdims=True))

    def weigh(s, m):
        return jnp.concatenate(
            [jnp.exp2(s[:, i * HD : (i + 1) * HD] - m) for i in range(s.shape[1] // HD)], axis=1
        )

    def p2_text(h, w):
        for t in range(2):
            rs = pl.ds(t * TT, TT)
            p = weigh(s_s[w, t, nb, :, :TEXT], m_ref[rs, hs(h)])
            l_ref[rs, hs(h)] = fold(p, jnp.add)
            v = t_ref[:, pl.ds(2 * W + h * HD, HD)]
            acc_ref[rs, hs(h)] = jnp.dot(p.astype(BF16), v, preferred_element_type=F32)

    def p2(h, w, b):
        v = kbuf[b, ROWS:, hs(h)]
        for t in range(2):
            rs = pl.ds(t * TT, TT)
            p = weigh(s_s[w, t, b], m_ref[rs, hs(h)])
            l_ref[rs, hs(h)] += fold(p, jnp.add)
            acc_ref[rs, hs(h)] += jnp.dot(p.astype(BF16), v, preferred_element_type=F32)

    p1_text(0, 0)
    for b in range(nb):
        pltpu.make_async_copy(blocks[b], kbuf.at[b], sem.at[b]).wait()
        p1(0, 0, b)
    top(0, 0)
    for h in range(NH):
        w = h % 2
        p2_text(h, w)
        if h + 1 < NH:
            p1_text(h + 1, 1 - w)
        for b in range(nb):
            p2(h, w, b)
            if h + 1 < NH:
                p1(h + 1, 1 - w, b)
        if h + 1 < NH:
            top(h + 1, 1 - w)


def early(wm, tlen, q, every, blocks):
    nb = len(blocks)
    part = jax.ShapeDtypeStruct((ROWS, W), F32)
    return pl.pallas_call(
        early_kernel,
        out_shape=(part, part, part),
        in_specs=[SM, SM, VM, VM] + [ANY] * nb,
        out_specs=(VM, VM, VM),
        scratch_shapes=[
            pltpu.VMEM((nb, 2 * ROWS, W), BF16),
            pltpu.VMEM((2, 2, nb + 1, TT, ROWS), F32),
            pltpu.VMEM((2, 2, TT, HD), F32),
            pltpu.SemaphoreType.DMA((nb,)),
        ],
        compiler_params=params(60),
        cost_estimate=cost(4 * ROWS * (nb * ROWS + TEXT) * W, 8 * 2**20, ROWS * nb * ROWS * NH),
        name="early",
    )(wm, tlen, q, every, *blocks)


def late_kernel(t, wm, q_ref, b0, b1, b2, acc_ref, m_ref, l_ref, o_ref):
    blocks = (b0, b1, b2)
    fcol = 2 * lax.rem(lax.axis_index("tile"), 2)
    rowof = (1, 0, 2)
    parts = []
    mx = None
    for b in range(3):
        s = scores(q_ref[...], blocks[b][:ROWS, :])
        for f in range(2):
            sf = s[:, f * TT : (f + 1) * TT] * SCALE + bias_of(wm, t, f, rowof[b], fcol)
            parts.append(sf)
            fx = fold(sf, jnp.maximum)
            mx = fx if mx is None else jnp.maximum(mx, fx)
    mo = m_ref[...]
    mn = jnp.maximum(mo, spread(jnp.max(mx, axis=1, keepdims=True)))
    al = jnp.exp2(mo - mn)
    acc = acc_ref[...] * al
    tot = l_ref[...] * al
    for b in range(3):
        p = jnp.concatenate(
            [
                jnp.exp2(parts[2 * b + f][:, i * HD : (i + 1) * HD] - mn)
                for f in range(2)
                for i in range(2)
            ],
            axis=1,
        )
        tot += fold(p, jnp.add)
        acc += jnp.dot(p.astype(BF16), blocks[b][ROWS:, :], preferred_element_type=F32)
    o = (acc / jnp.sum(tot, axis=1, keepdims=True)).astype(BF16)
    if t == 0:
        for x in range(4):
            o_ref[x] = o
    else:
        o_ref[...] = o


def late(t, wm, q, far, acc, m, l):
    head = pl.BlockSpec((TT, HD), lambda i: (t, i))
    block = pl.BlockSpec((2 * ROWS, HD), lambda i: (0, i))
    if t == 0:
        shape, out = (4, TT, W), pl.BlockSpec((4, TT, HD), lambda i: (0, 0, i))
    else:
        shape, out = (TT, W), pl.BlockSpec((TT, HD), lambda i: (0, i))
    return pl.pallas_call(
        functools.partial(late_kernel, t),
        grid=(NH,),
        out_shape=jax.ShapeDtypeStruct(shape, BF16),
        in_specs=[SM, head, block, block, block, head, head, head],
        out_specs=out,
        compiler_params=params(60),
        cost_estimate=cost(6 * ROWS * ROWS * W, 2 * 2**20, 3 * ROWS * TT),
        name="late",
    )(wm, q, *far, acc, m, l)


def columns(xd, j):
    z = lax.axis_index("head") // 4
    return pl.ds(pl.multiple_of(((z + j - 2 * j * z) * 4 + xd) * W, HD), W)


def pieces3(x):
    hi = x.astype(BF16).astype(F32)
    mid = (x - hi).astype(BF16).astype(F32)
    return hi, mid, x - hi - mid


def text_kernel(t_ref, kv_ref, *rest):
    msg_ref = rest[-1]
    lane = lax.broadcasted_iota(jnp.int32, (TEXT, HD), 1)
    stat = jnp.zeros((TEXT, HD), F32)
    for h in range(NH):
        hs = pl.ds(h * HD, HD)
        s = scores(t_ref[:, hs], kv_ref[:ROWS, hs]) * SCALE
        m = jnp.max(fold(s, jnp.maximum), axis=1, keepdims=True)
        p = jnp.exp2(s - m)
        tot = jnp.sum(fold(p, jnp.add), axis=1, keepdims=True)
        acc = jnp.dot(p.astype(BF16), kv_ref[ROWS:, hs], preferred_element_type=F32)
        msg_ref[:, hs] = (acc / tot).astype(BF16)
        for j, piece in enumerate(pieces3(m + jnp.log2(tot))):
            stat = jnp.where(lane == 8 * j + h, spread(piece), stat)
    msg_ref[:, W:] = stat.astype(BF16)


def text_part(every, kv, *deps):
    return pl.pallas_call(
        text_kernel,
        out_shape=jax.ShapeDtypeStruct((TEXT, W + HD), BF16),
        in_specs=[VM, VM] + [ANY] * len(deps),
        out_specs=VM,
        compiler_params=params(60),
        cost_estimate=cost(4 * TEXT * ROWS * W, 2 * 2**20, TEXT * ROWS * NH),
        name="text_part",
    )(every, kv, *deps)


def merge_kernel(tlen, msg_ref, tq_ref, t_ref, proj_ref, o0, o1, o2, o3, flat):
    msg = msg_ref[...].astype(F32)
    stat = msg[:, W:]
    slane = lax.broadcasted_iota(jnp.int32, (TEXT, HD), 1)
    lane = lax.broadcasted_iota(jnp.int32, (1, TEXT), 1)
    tbias = jnp.where(lane < tlen[0], 0.0, -BIG)
    q = tq_ref[...]
    attn = []
    for h in range(NH):
        hs = slice(h * HD, (h + 1) * HD)
        s = scores(q[:, hs], t_ref[:, pl.ds(W + h * HD, HD)]) * SCALE + tbias
        m = jnp.max(s, axis=1, keepdims=True)
        p = jnp.exp2(s - m)
        tot = jnp.sum(p, axis=1, keepdims=True)
        own = jnp.dot(p.astype(BF16), t_ref[:, pl.ds(2 * W + h * HD, HD)], preferred_element_type=F32)
        mine = (slane == h) | (slane == 8 + h) | (slane == 16 + h)
        lse = jnp.sum(jnp.where(mine, stat, 0.0), axis=1, keepdims=True)
        lse = spread(lse).reshape(TEXT // TL, TL, HD)
        peak = jnp.maximum(jnp.max(lse, axis=0), spread(m))
        wt = jnp.exp2(lse - peak[None])
        w0 = jnp.exp2(spread(m) - peak)
        num = jnp.sum(wt * msg[:, hs].reshape(TEXT // TL, TL, HD), axis=0) + w0 * own
        den = jnp.sum(wt, axis=0) + w0 * tot
        attn.append((num / den).astype(BF16))
    a = jnp.concatenate(attn, axis=1)
    flat[...] = jnp.dot(a, proj_ref[...], preferred_element_type=F32)
    x = lax.rem(lax.axis_index("head"), 4)
    for d, out in enumerate((o0, o1, o2, o3)):
        for j in range(2):
            cs = columns(lax.rem(x + d, 4), j)
            out[:, j * W : (j + 1) * W] = flat[:, cs].astype(BF16)


def text_merge(tlen, msg, tq, every, proj):
    return pl.pallas_call(
        merge_kernel,
        out_shape=(jax.ShapeDtypeStruct((TL, 2 * W), BF16),) * 4,
        in_specs=[SM, VM, VM, VM, VM],
        out_specs=(VM,) * 4,
        scratch_shapes=[pltpu.VMEM((TL, 8 * W), F32)],
        compiler_params=params(60),
        cost_estimate=cost(2 * TL * W * 8 * W, 3 * 2**20, TEXT * HD * NH),
        name="text_merge",
    )(tlen, msg, tq, every, proj)


def split_kernel(proj_ref, after_ref, out_ref):
    core = lax.rem(lax.axis_index("tile"), 2)
    mine = pl.ds(pl.multiple_of(core * HALF, 16), HALF)
    for xd in range(4):
        for j in range(2):
            out_ref[xd, :, j * W : (j + 1) * W] = proj_ref[mine, columns(xd, j)]


def split_proj(proj, after_this):
    return pl.pallas_call(
        split_kernel,
        out_shape=jax.ShapeDtypeStruct((4, HALF, 2 * W), BF16),
        in_specs=[VM, ANY],
        out_specs=VM,
        compiler_params=params(60),
        cost_estimate=cost(0, 5 * 2**20),
        name="split_proj",
    )(proj, after_this)


def pack_kernel(k_ref, v_ref, tq_ref, tk_ref, tv_ref, kv_ref, t_ref, buf, sem):
    copies = [
        pltpu.make_async_copy(r, d, sem.at[i])
        for i, (r, d) in enumerate(
            (
                (k_ref, kv_ref.at[pl.ds(0, ROWS)]),
                (v_ref, kv_ref.at[pl.ds(ROWS, ROWS)]),
                (tq_ref, buf.at[0]),
                (tk_ref, buf.at[1]),
                (tv_ref, buf.at[2]),
            )
        )
    ]
    for c in copies:
        c.start()
    for c in copies[2:]:
        c.wait()
    both = jnp.concatenate([buf[i] for i in range(3)], axis=1)
    for i in range(32):
        t_ref[i] = both
    for c in copies[:2]:
        c.wait()


def pack(k, v, tq, tk, tv):
    return pl.pallas_call(
        pack_kernel,
        out_shape=(
            jax.ShapeDtypeStruct((2 * ROWS, W), BF16),
            jax.ShapeDtypeStruct((32, TL, 3 * W), BF16),
        ),
        in_specs=[HBM] * 5,
        out_specs=(VM, VM),
        scratch_shapes=[pltpu.VMEM((3, TL, W), BF16), pltpu.SemaphoreType.DMA((5,))],
        compiler_params=params(60),
        cost_estimate=cost(0, 2 * 2**20),
        name="pack",
    )(k, v, tq, tk, tv)


def after_kernel(x_ref, *rest):
    pass


def after(x, *deps):
    return pl.pallas_call(
        after_kernel,
        out_shape=jax.ShapeDtypeStruct(x.shape, x.dtype),
        in_specs=[ANY] * (1 + len(deps)),
        out_specs=ANY,
        input_output_aliases={0: 0},
        compiler_params=params(60),
        cost_estimate=cost(0, 1),
        name="after",
    )(x, *deps)


def project_kernel(t, *refs):
    if t == 0:
        (a_ref, w_ref, v_ref), rest = refs[:3], refs[3:]
        order = [(a_ref.at[x], x) for x in range(4)]
    else:
        me = lax.rem(lax.axis_index("head"), 4)
        (w_ref, v_ref), rest = refs[4:6], refs[6:]
        order = [(refs[d], lax.rem(me + 4 - d, 4)) for d in range(4)]
    own_ref, away_ref, abuf, wbuf, acc, sem = rest[-6:]
    core = lax.rem(lax.axis_index("tile"), 2)
    copies = []
    for i, (a, x) in enumerate(order):
        for j, (src, dst) in enumerate(
            (
                (w_ref.at[x], wbuf.at[i, pl.ds(pl.multiple_of(core * HALF, 16), HALF)]),
                (v_ref.at[x], wbuf.at[i, pl.ds(pl.multiple_of((1 - core) * HALF, 16), HALF)]),
                (a, abuf.at[i]),
            )
        ):
            copies.append(pltpu.make_async_copy(src, dst, sem.at[3 * i + j]))
            copies[-1].start()
    if t == 1:
        text = sum(r[...].astype(F32) for r in rest[:4])
        text = jnp.concatenate([text, jnp.zeros_like(text)], axis=0)
        own_ref[pl.ds(TT, 16), :] = text[:, :W]
        away_ref[pl.ds(TT, 16), :] = text[:, W:].astype(BF16)
    for i in range(4):
        for c in copies[3 * i : 3 * i + 3]:
            c.wait()
        o = jnp.dot(abuf[i], wbuf[i], preferred_element_type=F32)
        if i > 0:
            o += acc[...]
        if i < 3:
            acc[...] = o
        else:
            own_ref[:TT, :] = o[:, :W]
            away_ref[:TT, :] = o[:, W:].astype(BF16)


def project(t, attn, proj, text=(), deps=()):
    rows = TT + 16 * t
    return pl.pallas_call(
        functools.partial(project_kernel, t),
        out_shape=(
            jax.ShapeDtypeStruct((rows, W), F32),
            jax.ShapeDtypeStruct((rows, W), BF16),
        ),
        in_specs=[ANY] * (len(attn) + 2) + [VM] * len(text) + [ANY] * len(deps),
        out_specs=(VM, VM),
        scratch_shapes=[
            pltpu.VMEM((4, TT, W), BF16),
            pltpu.VMEM((4, W, 2 * W), BF16),
            pltpu.VMEM((TT, 2 * W), F32),
            pltpu.SemaphoreType.DMA((12,)),
        ],
        compiler_params=params(24),
        cost_estimate=cost(2 * TT * 4 * W * 2 * W, 6 * 2**20),
        name="project",
    )(*attn, *proj, *text, *deps)


def add_kernel(o0, g0, o1, g1, video_ref, text_ref):
    video_ref[:TT, :] = (o0[...] + g0[...].astype(F32)).astype(BF16)
    video_ref[TT:, :] = (o1[:TT, :] + g1[:TT, :].astype(F32)).astype(BF16)
    t = o1[pl.ds(TT, 16), :] + g1[pl.ds(TT, 16), :].astype(F32)
    text_ref[...] = t[:TL, :].astype(BF16)


def add_up(*parts):
    return pl.pallas_call(
        add_kernel,
        out_shape=(jax.ShapeDtypeStruct((ROWS, W), BF16), jax.ShapeDtypeStruct((TL, W), BF16)),
        in_specs=[VM] * 4,
        out_specs=(VM, VM),
        compiler_params=params(8),
        cost_estimate=cost(0, 2 * 2**20),
        name="add_up",
    )(*parts)


def per_device(
    video_q, video_k, video_v, text_q, text_k, text_v, video_proj, text_proj, window_mask, text_length
):
    kv, text = pack(video_k, video_v, text_q, text_k, text_v)
    far = over_chip(kv)
    up = rows_on(kv, 1)
    dn = rows_on(kv, -1)
    side = other_core(kv)

    every = lax.all_to_all(text, "tile", 0, 0, tiled=True).reshape(TEXT, 3 * W)
    far_up, far_dn = rows_on(far, 1), rows_on(far, -1)
    msg = text_part(every, kv)
    pieces = split_proj(video_proj, msg)
    proj = x_swap(pieces)
    up, dn = after(up, msg, pieces), after(dn, msg, pieces)
    side_up, side_dn = other_core(up), other_core(dn)
    acc, m, l = early(
        window_mask, text_length, video_q, every, (kv, up, dn, side, side_up, side_dn)
    )
    msg = after(msg.reshape(32, TL, W + HD), acc)
    got = lax.all_to_all(msg, "tile", 0, 0, tiled=True).reshape(TEXT, W + HD)

    given = (window_mask, video_q, (far, far_up, far_dn), acc, m, l)
    first = x_swap(late(0, *given))
    second = late(1, *given)
    second = [x_on(second, d) if d else second for d in range(4)]
    parts = text_merge(text_length, got, text_q, every, text_proj)
    parts = [x_on(p, d) if d else p for d, p in enumerate(parts)]
    proj = (proj, other_core(proj))
    own0, away0 = project(0, [first], proj)
    own1, away1 = project(1, second, proj, parts, (away0,))
    return add_up(own0, z_pair(away0), own1, z_pair(away1))


def solution(mesh):
    both, rows = P("tile", "head"), P("head", None)
    return jax.shard_map(
        per_device,
        mesh=mesh,
        in_specs=(both,) * 6 + (rows, rows, P("tile", None), P()),
        out_specs=(both, both),
        check_vma=False,
    )
```

```python
import functools
import math

import jax
import jax.numpy as jnp
from jax import lax
from jax.experimental import pallas as pl
from jax.experimental.pallas import tpu as pltpu
from jax.sharding import PartitionSpec as P

HD = 128
TT = 256
NH = 3
W = NH * HD
TEXT = 256
TL = 8
ROWS = 2 * TT
SCALE = math.log2(math.e) / math.sqrt(HD)
HALF = W // 2
BIG = 1e30
F32 = jnp.float32
BF16 = jnp.bfloat16

ANY = pl.BlockSpec(memory_space=pl.ANY)
SM = pl.BlockSpec(memory_space=pltpu.SMEM)
VM = pl.BlockSpec(memory_space=pltpu.VMEM)
HBM = pl.BlockSpec(memory_space=pltpu.HBM)


def params(mib):
    return pltpu.CompilerParams(vmem_limit_bytes=mib * 2**20)


def cost(flops, nbytes, exps=0):
    return pl.CostEstimate(flops=1, bytes_accessed=1, transcendentals=1)


def rows_on(x, d):
    return lax.ppermute(x, "tile", [(i, ((i // 8 + d) % 4) * 8 + i % 8) for i in range(32)])


def over_chip(x):
    return lax.ppermute(
        x, "tile", [(i, (i // 8) * 8 + (i % 8 + (1 if i % 2 else -1)) % 8) for i in range(32)]
    )


def other_core(x):
    return lax.ppermute(x, "tile", [(i, i ^ 1) for i in range(32)])


def x_swap(x):
    groups = [[0, 1, 2, 3], [4, 5, 6, 7]]
    return lax.all_to_all(x, "head", 0, 0, tiled=True, axis_index_groups=groups)


def x_on(x, d):
    return lax.ppermute(x, "head", [(i, (i // 4) * 4 + (i + d) % 4) for i in range(8)])


def z_pair(x):
    return lax.ppermute(x, "head", [(i, i ^ 4) for i in range(8)])


def fold(x, op):
    r = x[:, :HD]
    for i in range(1, x.shape[1] // HD):
        r = op(r, x[:, i * HD : (i + 1) * HD])
    return r


def scores(q, k):
    return lax.dot_general(q, k, (((1,), (1,)), ((), ())), preferred_element_type=F32)


def spread(col):
    return jnp.broadcast_to(col, (col.shape[0], HD))


def bias_of(wm, tile, frame, row, col):
    live = wm[tile, 9 * (frame - tile + 1) + 3 * row + col]
    return jnp.where(live > 0, 0.0, -BIG).astype(F32)


def early_kernel(
    wm, tlen, q_ref, t_ref, b0, b1, b2, b3, b4, b5, acc_ref, m_ref, l_ref, kbuf, s_s, mx_s, sem
):
    blocks = (b0, b1, b2, b3, b4, b5)
    nb = len(blocks)
    for b in range(nb):
        pltpu.make_async_copy(blocks[b], kbuf.at[b], sem.at[b]).start()
    lane = lax.broadcasted_iota(jnp.int32, (1, TEXT), 1)
    tbias = jnp.where(lane < tlen[0], 0.0, -BIG)
    pcol = 2 - 2 * lax.rem(lax.axis_index("tile"), 2)
    colof = (1, 1, 1, pcol, pcol, pcol)
    rowof = (1, 0, 2, 1, 0, 2)

    def hs(h):
        return pl.ds(h * HD, HD)

    def p1_text(h, w):
        for t in range(2):
            k = t_ref[:, pl.ds(W + h * HD, HD)]
            s = scores(q_ref[pl.ds(t * TT, TT), hs(h)], k) * SCALE + tbias
            s_s[w, t, nb, :, :TEXT] = s
            mx_s[w, t] = fold(s, jnp.maximum)

    def p1(h, w, b):
        k = kbuf[b, :ROWS, hs(h)]
        for t in range(2):
            s = scores(q_ref[pl.ds(t * TT, TT), hs(h)], k)
            mx = mx_s[w, t]
            for f in range(2):
                sf = s[:, f * TT : (f + 1) * TT] * SCALE + bias_of(wm, t, f, rowof[b], colof[b])
                s_s[w, t, b, :, f * TT : (f + 1) * TT] = sf
                mx = jnp.maximum(mx, fold(sf, jnp.maximum))
            mx_s[w, t] = mx

    def top(h, w):
        for t in range(2):
            m_ref[pl.ds(t * TT, TT), hs(h)] = spread(jnp.max(mx_s[w, t], axis=1, keepdims=True))

    def weigh(s, m):
        return jnp.concatenate(
            [jnp.exp2(s[:, i * HD : (i + 1) * HD] - m) for i in range(s.shape[1] // HD)], axis=1
        )

    def p2_text(h, w):
        for t in range(2):
            rs = pl.ds(t * TT, TT)
            p = weigh(s_s[w, t, nb, :, :TEXT], m_ref[rs, hs(h)])
            l_ref[rs, hs(h)] = fold(p, jnp.add)
            v = t_ref[:, pl.ds(2 * W + h * HD, HD)]
            acc_ref[rs, hs(h)] = jnp.dot(p.astype(BF16), v, preferred_element_type=F32)

    def p2(h, w, b):
        v = kbuf[b, ROWS:, hs(h)]
        for t in range(2):
            rs = pl.ds(t * TT, TT)
            p = weigh(s_s[w, t, b], m_ref[rs, hs(h)])
            l_ref[rs, hs(h)] += fold(p, jnp.add)
            acc_ref[rs, hs(h)] += jnp.dot(p.astype(BF16), v, preferred_element_type=F32)

    p1_text(0, 0)
    for b in range(nb):
        pltpu.make_async_copy(blocks[b], kbuf.at[b], sem.at[b]).wait()
        p1(0, 0, b)
    top(0, 0)
    for h in range(NH):
        w = h % 2
        p2_text(h, w)
        if h + 1 < NH:
            p1_text(h + 1, 1 - w)
        for b in range(nb):
            p2(h, w, b)
            if h + 1 < NH:
                p1(h + 1, 1 - w, b)
        if h + 1 < NH:
            top(h + 1, 1 - w)


def early(wm, tlen, q, every, blocks):
    nb = len(blocks)
    part = jax.ShapeDtypeStruct((ROWS, W), F32)
    return pl.pallas_call(
        early_kernel,
        out_shape=(part, part, part),
        in_specs=[SM, SM, VM, VM] + [ANY] * nb,
        out_specs=(VM, VM, VM),
        scratch_shapes=[
            pltpu.VMEM((nb, 2 * ROWS, W), BF16),
            pltpu.VMEM((2, 2, nb + 1, TT, ROWS), F32),
            pltpu.VMEM((2, 2, TT, HD), F32),
            pltpu.SemaphoreType.DMA((nb,)),
        ],
        compiler_params=params(60),
        cost_estimate=cost(4 * ROWS * (nb * ROWS + TEXT) * W, 8 * 2**20, ROWS * nb * ROWS * NH),
        name="early",
    )(wm, tlen, q, every, *blocks)


def late_kernel(wm, q_ref, b0, b1, b2, acc_ref, m_ref, l_ref, *rest):
    o_ref = rest[-1]
    blocks = (b0, b1, b2)
    fcol = 2 * lax.rem(lax.axis_index("tile"), 2)
    rowof = (1, 0, 2)
    for t in range(2):
        rs = pl.ds(t * TT, TT)
        parts = []
        mx = None
        for b in range(3):
            s = scores(q_ref[rs, :], blocks[b][:ROWS, :])
            for f in range(2):
                sf = s[:, f * TT : (f + 1) * TT] * SCALE + bias_of(wm, t, f, rowof[b], fcol)
                parts.append(sf)
                fx = fold(sf, jnp.maximum)
                mx = fx if mx is None else jnp.maximum(mx, fx)
        mo = m_ref[rs, :]
        mn = jnp.maximum(mo, spread(jnp.max(mx, axis=1, keepdims=True)))
        al = jnp.exp2(mo - mn)
        acc = acc_ref[rs, :] * al
        tot = l_ref[rs, :] * al
        for b in range(3):
            p = jnp.concatenate(
                [
                    jnp.exp2(parts[2 * b + f][:, i * HD : (i + 1) * HD] - mn)
                    for f in range(2)
                    for i in range(2)
                ],
                axis=1,
            )
            tot += fold(p, jnp.add)
            acc += jnp.dot(p.astype(BF16), blocks[b][ROWS:, :], preferred_element_type=F32)
        o = (acc / jnp.sum(tot, axis=1, keepdims=True)).astype(BF16)
        for x in range(4):
            o_ref[x, rs, :] = o


def late(wm, q, far, acc, m, l, *deps):
    head = pl.BlockSpec((ROWS, HD), lambda i: (0, i))
    block = pl.BlockSpec((2 * ROWS, HD), lambda i: (0, i))
    return pl.pallas_call(
        late_kernel,
        grid=(NH,),
        out_shape=jax.ShapeDtypeStruct((4, ROWS, W), BF16),
        in_specs=[SM, head, block, block, block, head, head, head] + [ANY] * len(deps),
        out_specs=pl.BlockSpec((4, ROWS, HD), lambda i: (0, 0, i)),
        compiler_params=params(60),
        cost_estimate=cost(12 * ROWS * ROWS * W, 2 * 2**20, 3 * ROWS * ROWS),
        name="late",
    )(wm, q, *far, acc, m, l, *deps)


def columns(xd, j):
    z = lax.axis_index("head") // 4
    return pl.ds(pl.multiple_of(((z + j - 2 * j * z) * 4 + xd) * W, HD), W)


def pieces3(x):
    hi = x.astype(BF16).astype(F32)
    mid = (x - hi).astype(BF16).astype(F32)
    return hi, mid, x - hi - mid


def text_kernel(t_ref, kv_ref, *rest):
    msg_ref = rest[-1]
    lane = lax.broadcasted_iota(jnp.int32, (TEXT, HD), 1)
    stat = jnp.zeros((TEXT, HD), F32)
    for h in range(NH):
        hs = pl.ds(h * HD, HD)
        s = scores(t_ref[:, hs], kv_ref[:ROWS, hs]) * SCALE
        m = jnp.max(fold(s, jnp.maximum), axis=1, keepdims=True)
        p = jnp.exp2(s - m)
        tot = jnp.sum(fold(p, jnp.add), axis=1, keepdims=True)
        acc = jnp.dot(p.astype(BF16), kv_ref[ROWS:, hs], preferred_element_type=F32)
        msg_ref[:, hs] = (acc / tot).astype(BF16)
        for j, piece in enumerate(pieces3(m + jnp.log2(tot))):
            stat = jnp.where(lane == 8 * j + h, spread(piece), stat)
    msg_ref[:, W:] = stat.astype(BF16)


def text_part(every, kv, *deps):
    return pl.pallas_call(
        text_kernel,
        out_shape=jax.ShapeDtypeStruct((TEXT, W + HD), BF16),
        in_specs=[VM, VM] + [ANY] * len(deps),
        out_specs=VM,
        compiler_params=params(60),
        cost_estimate=cost(4 * TEXT * ROWS * W, 2 * 2**20, TEXT * ROWS * NH),
        name="text_part",
    )(every, kv, *deps)


def merge_kernel(tlen, msg_ref, tq_ref, t_ref, proj_ref, o0, o1, o2, o3, flat):
    msg = msg_ref[...].astype(F32)
    stat = msg[:, W:]
    slane = lax.broadcasted_iota(jnp.int32, (TEXT, HD), 1)
    lane = lax.broadcasted_iota(jnp.int32, (1, TEXT), 1)
    tbias = jnp.where(lane < tlen[0], 0.0, -BIG)
    q = tq_ref[...]
    attn = []
    for h in range(NH):
        hs = slice(h * HD, (h + 1) * HD)
        s = scores(q[:, hs], t_ref[:, pl.ds(W + h * HD, HD)]) * SCALE + tbias
        m = jnp.max(s, axis=1, keepdims=True)
        p = jnp.exp2(s - m)
        tot = jnp.sum(p, axis=1, keepdims=True)
        own = jnp.dot(p.astype(BF16), t_ref[:, pl.ds(2 * W + h * HD, HD)], preferred_element_type=F32)
        mine = (slane == h) | (slane == 8 + h) | (slane == 16 + h)
        lse = jnp.sum(jnp.where(mine, stat, 0.0), axis=1, keepdims=True)
        lse = spread(lse).reshape(TEXT // TL, TL, HD)
        peak = jnp.maximum(jnp.max(lse, axis=0), spread(m))
        wt = jnp.exp2(lse - peak[None])
        w0 = jnp.exp2(spread(m) - peak)
        num = jnp.sum(wt * msg[:, hs].reshape(TEXT // TL, TL, HD), axis=0) + w0 * own
        den = jnp.sum(wt, axis=0) + w0 * tot
        attn.append((num / den).astype(BF16))
    a = jnp.concatenate(attn, axis=1)
    flat[...] = jnp.dot(a, proj_ref[...], preferred_element_type=F32)
    x = lax.rem(lax.axis_index("head"), 4)
    for d, out in enumerate((o0, o1, o2, o3)):
        for j in range(2):
            cs = columns(lax.rem(x + d, 4), j)
            out[:, j * W : (j + 1) * W] = flat[:, cs].astype(BF16)


def text_merge(tlen, msg, tq, every, proj):
    return pl.pallas_call(
        merge_kernel,
        out_shape=(jax.ShapeDtypeStruct((TL, 2 * W), BF16),) * 4,
        in_specs=[SM, VM, VM, VM, VM],
        out_specs=(VM,) * 4,
        scratch_shapes=[pltpu.VMEM((TL, 8 * W), F32)],
        compiler_params=params(60),
        cost_estimate=cost(2 * TL * W * 8 * W, 3 * 2**20, TEXT * HD * NH),
        name="text_merge",
    )(tlen, msg, tq, every, proj)


def split_kernel(proj_ref, after_ref, out_ref):
    core = lax.rem(lax.axis_index("tile"), 2)
    mine = pl.ds(pl.multiple_of(core * HALF, 16), HALF)
    for xd in range(4):
        for j in range(2):
            out_ref[xd, :, j * W : (j + 1) * W] = proj_ref[mine, columns(xd, j)]


def split_proj(proj, after_this):
    return pl.pallas_call(
        split_kernel,
        out_shape=jax.ShapeDtypeStruct((4, HALF, 2 * W), BF16),
        in_specs=[VM, ANY],
        out_specs=VM,
        compiler_params=params(60),
        cost_estimate=cost(0, 5 * 2**20),
        name="split_proj",
    )(proj, after_this)


def pack_kernel(k_ref, v_ref, tq_ref, tk_ref, tv_ref, kv_ref, t_ref, buf, sem):
    copies = [
        pltpu.make_async_copy(r, d, sem.at[i])
        for i, (r, d) in enumerate(
            (
                (k_ref, kv_ref.at[pl.ds(0, ROWS)]),
                (v_ref, kv_ref.at[pl.ds(ROWS, ROWS)]),
                (tq_ref, buf.at[0]),
                (tk_ref, buf.at[1]),
                (tv_ref, buf.at[2]),
            )
        )
    ]
    for c in copies:
        c.start()
    for c in copies[2:]:
        c.wait()
    both = jnp.concatenate([buf[i] for i in range(3)], axis=1)
    for i in range(32):
        t_ref[i] = both
    for c in copies[:2]:
        c.wait()


def pack(k, v, tq, tk, tv):
    return pl.pallas_call(
        pack_kernel,
        out_shape=(
            jax.ShapeDtypeStruct((2 * ROWS, W), BF16),
            jax.ShapeDtypeStruct((32, TL, 3 * W), BF16),
        ),
        in_specs=[HBM] * 5,
        out_specs=(VM, VM),
        scratch_shapes=[pltpu.VMEM((3, TL, W), BF16), pltpu.SemaphoreType.DMA((5,))],
        compiler_params=params(60),
        cost_estimate=cost(0, 2 * 2**20),
        name="pack",
    )(k, v, tq, tk, tv)


def after_kernel(x_ref, *rest):
    pass


def after(x, *deps, mib=60):
    return pl.pallas_call(
        after_kernel,
        out_shape=jax.ShapeDtypeStruct(x.shape, x.dtype),
        in_specs=[ANY] * (1 + len(deps)),
        out_specs=ANY,
        input_output_aliases={0: 0},
        compiler_params=params(mib),
        cost_estimate=cost(0, 1),
        name="after",
    )(x, *deps)


def project_kernel(
    a_ref, w_ref, v_ref, t0, t1, t2, t3, own_ref, away_ref, abuf, wbuf, acc, sem
):
    core = lax.rem(lax.axis_index("tile"), 2)
    copies = []
    for x in range(4):
        for i, (src, dst) in enumerate(
            (
                (w_ref, wbuf.at[x, pl.ds(pl.multiple_of(core * HALF, 16), HALF)]),
                (v_ref, wbuf.at[x, pl.ds(pl.multiple_of((1 - core) * HALF, 16), HALF)]),
                (a_ref, abuf.at[x]),
            )
        ):
            copies.append(pltpu.make_async_copy(src.at[x], dst, sem.at[3 * x + i]))
            copies[-1].start()
    t = sum(r[...].astype(F32) for r in (t0, t1, t2, t3))
    t = jnp.concatenate([t, jnp.zeros_like(t)], axis=0)
    own_ref[pl.ds(ROWS, 16), :] = t[:, :W]
    away_ref[pl.ds(ROWS, 16), :] = t[:, W:].astype(BF16)
    for x in range(4):
        for c in copies[3 * x : 3 * x + 3]:
            c.wait()
        o = jnp.dot(abuf[x], wbuf[x], preferred_element_type=F32)
        if x > 0:
            o += acc[...]
        if x < 3:
            acc[...] = o
        else:
            own_ref[:ROWS, :] = o[:, :W]
            away_ref[:ROWS, :] = o[:, W:].astype(BF16)


def project(attn, proj, text):
    return pl.pallas_call(
        project_kernel,
        out_shape=(
            jax.ShapeDtypeStruct((ROWS + 16, W), F32),
            jax.ShapeDtypeStruct((ROWS + 16, W), BF16),
        ),
        in_specs=[ANY] * 3 + [VM] * 4,
        out_specs=(VM, VM),
        scratch_shapes=[
            pltpu.VMEM((4, ROWS, W), BF16),
            pltpu.VMEM((4, W, 2 * W), BF16),
            pltpu.VMEM((ROWS, 2 * W), F32),
            pltpu.SemaphoreType.DMA((12,)),
        ],
        compiler_params=params(24),
        cost_estimate=cost(2 * ROWS * 4 * W * 2 * W, 6 * 2**20),
        name="project",
    )(attn, *proj, *text)


def add_kernel(own_ref, got_ref, video_ref, text_ref):
    video_ref[...] = (own_ref[:ROWS, :] + got_ref[:ROWS, :].astype(F32)).astype(BF16)
    t = own_ref[pl.ds(ROWS, 16), :] + got_ref[pl.ds(ROWS, 16), :].astype(F32)
    text_ref[...] = t[:TL, :].astype(BF16)


def add_up(own, got):
    return pl.pallas_call(
        add_kernel,
        out_shape=(jax.ShapeDtypeStruct((ROWS, W), BF16), jax.ShapeDtypeStruct((TL, W), BF16)),
        in_specs=[VM, VM],
        out_specs=(VM, VM),
        compiler_params=params(8),
        cost_estimate=cost(0, 2 * 2**20),
        name="add_up",
    )(own, got)


def per_device(
    video_q, video_k, video_v, text_q, text_k, text_v, video_proj, text_proj, window_mask, text_length
):
    kv, text = pack(video_k, video_v, text_q, text_k, text_v)
    far = over_chip(kv)
    up = rows_on(kv, 1)
    dn = rows_on(kv, -1)
    side = other_core(kv)

    every = lax.all_to_all(text, "tile", 0, 0, tiled=True).reshape(TEXT, 3 * W)
    far_up, far_dn = rows_on(far, 1), rows_on(far, -1)
    msg = text_part(every, kv)
    pieces = split_proj(video_proj, side)
    proj = x_swap(pieces)
    up, dn = (after(r, msg, pieces, mib=1) for r in (up, dn))
    side_up, side_dn = other_core(up), other_core(dn)
    acc, m, l = early(
        window_mask, text_length, video_q, every, (kv, up, dn, side, side_up, side_dn)
    )
    msg = after(msg.reshape(32, TL, W + HD), acc)
    got = lax.all_to_all(msg, "tile", 0, 0, tiled=True).reshape(TEXT, W + HD)

    attn = x_swap(late(window_mask, video_q, (far, far_up, far_dn), acc, m, l))
    parts = text_merge(text_length, got, text_q, every, text_proj)
    parts = [x_on(p, d) if d else p for d, p in enumerate(parts)]
    own, away = project(attn, (proj, other_core(proj)), parts)
    return add_up(own, z_pair(away))


def solution(mesh):
    both, rows = P("tile", "head"), P("head", None)
    return jax.shard_map(
        per_device,
        mesh=mesh,
        in_specs=(both,) * 6 + (rows, rows, P("tile", None), P()),
        out_specs=(both, both),
        check_vma=False,
    )
```

```python
import functools
import math

import jax
import jax.numpy as jnp
from jax import lax
from jax.experimental import pallas as pl
from jax.experimental.pallas import tpu as pltpu
from jax.sharding import PartitionSpec as P

HD = 128
TT = 256
NH = 3
W = NH * HD
TEXT = 256
TL = 8
ROWS = 2 * TT
SCALE = math.log2(math.e) / math.sqrt(HD)
HALF = W // 2
BIG = 1e30
F32 = jnp.float32
BF16 = jnp.bfloat16

ANY = pl.BlockSpec(memory_space=pl.ANY)
SM = pl.BlockSpec(memory_space=pltpu.SMEM)
VM = pl.BlockSpec(memory_space=pltpu.VMEM)
HBM = pl.BlockSpec(memory_space=pltpu.HBM)


def params(mib):
    return pltpu.CompilerParams(vmem_limit_bytes=mib * 2**20)


def cost(flops, nbytes, exps=0):
    return pl.CostEstimate(flops=1, bytes_accessed=1, transcendentals=1)


def rows_on(x, d):
    return lax.ppermute(x, "tile", [(i, ((i // 8 + d) % 4) * 8 + i % 8) for i in range(32)])


def over_chip(x):
    return lax.ppermute(
        x, "tile", [(i, (i // 8) * 8 + (i % 8 + (1 if i % 2 else -1)) % 8) for i in range(32)]
    )


def other_core(x):
    return lax.ppermute(x, "tile", [(i, i ^ 1) for i in range(32)])


def x_swap(x):
    groups = [[0, 1, 2, 3], [4, 5, 6, 7]]
    return lax.all_to_all(x, "head", 0, 0, tiled=True, axis_index_groups=groups)


def x_on(x, d):
    return lax.ppermute(x, "head", [(i, (i // 4) * 4 + (i + d) % 4) for i in range(8)])


def z_pair(x):
    return lax.ppermute(x, "head", [(i, i ^ 4) for i in range(8)])


def fold(x, op):
    r = x[:, :HD]
    for i in range(1, x.shape[1] // HD):
        r = op(r, x[:, i * HD : (i + 1) * HD])
    return r


def scores(q, k):
    return lax.dot_general(q, k, (((1,), (1,)), ((), ())), preferred_element_type=F32)


def spread(col):
    return jnp.broadcast_to(col, (col.shape[0], HD))


def bias_of(wm, tile, frame, row, col):
    live = wm[tile, 9 * (frame - tile + 1) + 3 * row + col]
    return jnp.where(live > 0, 0.0, -BIG).astype(F32)


def early_kernel(
    wm, tlen, q_ref, t_ref, b0, b1, b2, b3, b4, b5, acc_ref, m_ref, l_ref, kbuf, s_s, mx_s, sem
):
    blocks = (b0, b1, b2, b3, b4, b5)
    nb = len(blocks)
    for b in range(nb):
        pltpu.make_async_copy(blocks[b], kbuf.at[b], sem.at[b]).start()
    lane = lax.broadcasted_iota(jnp.int32, (1, TEXT), 1)
    tbias = jnp.where(lane < tlen[0], 0.0, -BIG)
    pcol = 2 - 2 * lax.rem(lax.axis_index("tile"), 2)
    colof = (1, 1, 1, pcol, pcol, pcol)
    rowof = (1, 0, 2, 1, 0, 2)

    def hs(h):
        return pl.ds(h * HD, HD)

    def p1_text(h, w):
        for t in range(2):
            k = t_ref[:, pl.ds(W + h * HD, HD)]
            s = scores(q_ref[pl.ds(t * TT, TT), hs(h)], k) * SCALE + tbias
            s_s[w, t, nb, :, :TEXT] = s
            mx_s[w, t] = fold(s, jnp.maximum)

    def p1(h, w, b):
        k = kbuf[b, :ROWS, hs(h)]
        for t in range(2):
            s = scores(q_ref[pl.ds(t * TT, TT), hs(h)], k)
            mx = mx_s[w, t]
            for f in range(2):
                sf = s[:, f * TT : (f + 1) * TT] * SCALE + bias_of(wm, t, f, rowof[b], colof[b])
                s_s[w, t, b, :, f * TT : (f + 1) * TT] = sf
                mx = jnp.maximum(mx, fold(sf, jnp.maximum))
            mx_s[w, t] = mx

    def top(h, w):
        for t in range(2):
            m_ref[pl.ds(t * TT, TT), hs(h)] = spread(jnp.max(mx_s[w, t], axis=1, keepdims=True))

    def weigh(s, m):
        return jnp.concatenate(
            [jnp.exp2(s[:, i * HD : (i + 1) * HD] - m) for i in range(s.shape[1] // HD)], axis=1
        )

    def p2_text(h, w):
        for t in range(2):
            rs = pl.ds(t * TT, TT)
            p = weigh(s_s[w, t, nb, :, :TEXT], m_ref[rs, hs(h)])
            l_ref[rs, hs(h)] = fold(p, jnp.add)
            v = t_ref[:, pl.ds(2 * W + h * HD, HD)]
            acc_ref[rs, hs(h)] = jnp.dot(p.astype(BF16), v, preferred_element_type=F32)

    def p2(h, w, b):
        v = kbuf[b, ROWS:, hs(h)]
        for t in range(2):
            rs = pl.ds(t * TT, TT)
            p = weigh(s_s[w, t, b], m_ref[rs, hs(h)])
            l_ref[rs, hs(h)] += fold(p, jnp.add)
            acc_ref[rs, hs(h)] += jnp.dot(p.astype(BF16), v, preferred_element_type=F32)

    p1_text(0, 0)
    for b in range(nb):
        pltpu.make_async_copy(blocks[b], kbuf.at[b], sem.at[b]).wait()
        p1(0, 0, b)
    top(0, 0)
    for h in range(NH):
        w = h % 2
        p2_text(h, w)
        if h + 1 < NH:
            p1_text(h + 1, 1 - w)
        for b in range(nb):
            p2(h, w, b)
            if h + 1 < NH:
                p1(h + 1, 1 - w, b)
        if h + 1 < NH:
            top(h + 1, 1 - w)


def early(wm, tlen, q, every, blocks):
    nb = len(blocks)
    part = jax.ShapeDtypeStruct((ROWS, W), F32)
    return pl.pallas_call(
        early_kernel,
        out_shape=(part, part, part),
        in_specs=[SM, SM, VM, VM] + [ANY] * nb,
        out_specs=(VM, VM, VM),
        scratch_shapes=[
            pltpu.VMEM((nb, 2 * ROWS, W), BF16),
            pltpu.VMEM((2, 2, nb + 1, TT, ROWS), F32),
            pltpu.VMEM((2, 2, TT, HD), F32),
            pltpu.SemaphoreType.DMA((nb,)),
        ],
        compiler_params=params(60),
        cost_estimate=cost(4 * ROWS * (nb * ROWS + TEXT) * W, 8 * 2**20, ROWS * nb * ROWS * NH),
        name="early",
    )(wm, tlen, q, every, *blocks)


def late_kernel(wm, q_ref, b0, b1, b2, acc_ref, m_ref, l_ref, *rest):
    o_ref = rest[-1]
    blocks = (b0, b1, b2)
    fcol = 2 * lax.rem(lax.axis_index("tile"), 2)
    rowof = (1, 0, 2)
    for t in range(2):
        rs = pl.ds(t * TT, TT)
        parts = []
        mx = None
        for b in range(3):
            s = scores(q_ref[rs, :], blocks[b][:ROWS, :])
            for f in range(2):
                sf = s[:, f * TT : (f + 1) * TT] * SCALE + bias_of(wm, t, f, rowof[b], fcol)
                parts.append(sf)
                fx = fold(sf, jnp.maximum)
                mx = fx if mx is None else jnp.maximum(mx, fx)
        mo = m_ref[rs, :]
        mn = jnp.maximum(mo, spread(jnp.max(mx, axis=1, keepdims=True)))
        al = jnp.exp2(mo - mn)
        acc = acc_ref[rs, :] * al
        tot = l_ref[rs, :] * al
        for b in range(3):
            p = jnp.concatenate(
                [
                    jnp.exp2(parts[2 * b + f][:, i * HD : (i + 1) * HD] - mn)
                    for f in range(2)
                    for i in range(2)
                ],
                axis=1,
            )
            tot += fold(p, jnp.add)
            acc += jnp.dot(p.astype(BF16), blocks[b][ROWS:, :], preferred_element_type=F32)
        o = (acc / jnp.sum(tot, axis=1, keepdims=True)).astype(BF16)
        o_ref[rs, :] = o


def late(wm, q, far, acc, m, l, *deps):
    head = pl.BlockSpec((ROWS, HD), lambda i: (0, i))
    block = pl.BlockSpec((2 * ROWS, HD), lambda i: (0, i))
    return pl.pallas_call(
        late_kernel,
        grid=(NH,),
        out_shape=jax.ShapeDtypeStruct((ROWS, W), BF16),
        in_specs=[SM, head, block, block, block, head, head, head] + [ANY] * len(deps),
        out_specs=head,
        compiler_params=params(60),
        cost_estimate=cost(12 * ROWS * ROWS * W, 2 * 2**20, 3 * ROWS * ROWS),
        name="late",
    )(wm, q, *far, acc, m, l, *deps)


def columns(xd, j):
    z = lax.axis_index("head") // 4
    return pl.ds(pl.multiple_of(((z + j - 2 * j * z) * 4 + xd) * W, HD), W)


def pieces3(x):
    hi = x.astype(BF16).astype(F32)
    mid = (x - hi).astype(BF16).astype(F32)
    return hi, mid, x - hi - mid


def text_kernel(t_ref, kv_ref, *rest):
    msg_ref = rest[-1]
    lane = lax.broadcasted_iota(jnp.int32, (TEXT, HD), 1)
    stat = jnp.zeros((TEXT, HD), F32)
    for h in range(NH):
        hs = pl.ds(h * HD, HD)
        s = scores(t_ref[:, hs], kv_ref[:ROWS, hs]) * SCALE
        m = jnp.max(fold(s, jnp.maximum), axis=1, keepdims=True)
        p = jnp.exp2(s - m)
        tot = jnp.sum(fold(p, jnp.add), axis=1, keepdims=True)
        acc = jnp.dot(p.astype(BF16), kv_ref[ROWS:, hs], preferred_element_type=F32)
        msg_ref[:, hs] = (acc / tot).astype(BF16)
        for j, piece in enumerate(pieces3(m + jnp.log2(tot))):
            stat = jnp.where(lane == 8 * j + h, spread(piece), stat)
    msg_ref[:, W:] = stat.astype(BF16)


def text_part(every, kv, *deps):
    return pl.pallas_call(
        text_kernel,
        out_shape=jax.ShapeDtypeStruct((TEXT, W + HD), BF16),
        in_specs=[VM, VM] + [ANY] * len(deps),
        out_specs=VM,
        compiler_params=params(60),
        cost_estimate=cost(4 * TEXT * ROWS * W, 2 * 2**20, TEXT * ROWS * NH),
        name="text_part",
    )(every, kv, *deps)


def merge_kernel(tlen, msg_ref, tq_ref, t_ref, proj_ref, o0, o1, o2, o3, flat):
    msg = msg_ref[...].astype(F32)
    stat = msg[:, W:]
    slane = lax.broadcasted_iota(jnp.int32, (TEXT, HD), 1)
    lane = lax.broadcasted_iota(jnp.int32, (1, TEXT), 1)
    tbias = jnp.where(lane < tlen[0], 0.0, -BIG)
    q = tq_ref[...]
    attn = []
    for h in range(NH):
        hs = slice(h * HD, (h + 1) * HD)
        s = scores(q[:, hs], t_ref[:, pl.ds(W + h * HD, HD)]) * SCALE + tbias
        m = jnp.max(s, axis=1, keepdims=True)
        p = jnp.exp2(s - m)
        tot = jnp.sum(p, axis=1, keepdims=True)
        own = jnp.dot(p.astype(BF16), t_ref[:, pl.ds(2 * W + h * HD, HD)], preferred_element_type=F32)
        mine = (slane == h) | (slane == 8 + h) | (slane == 16 + h)
        lse = jnp.sum(jnp.where(mine, stat, 0.0), axis=1, keepdims=True)
        lse = spread(lse).reshape(TEXT // TL, TL, HD)
        peak = jnp.maximum(jnp.max(lse, axis=0), spread(m))
        wt = jnp.exp2(lse - peak[None])
        w0 = jnp.exp2(spread(m) - peak)
        num = jnp.sum(wt * msg[:, hs].reshape(TEXT // TL, TL, HD), axis=0) + w0 * own
        den = jnp.sum(wt, axis=0) + w0 * tot
        attn.append((num / den).astype(BF16))
    a = jnp.concatenate(attn, axis=1)
    flat[...] = jnp.dot(a, proj_ref[...], preferred_element_type=F32)
    x = lax.rem(lax.axis_index("head"), 4)
    for d, out in enumerate((o0, o1, o2, o3)):
        for j in range(2):
            cs = columns(lax.rem(x + d, 4), j)
            out[:, j * W : (j + 1) * W] = flat[:, cs].astype(BF16)


def text_merge(tlen, msg, tq, every, proj):
    return pl.pallas_call(
        merge_kernel,
        out_shape=(jax.ShapeDtypeStruct((TL, 2 * W), BF16),) * 4,
        in_specs=[SM, VM, VM, VM, VM],
        out_specs=(VM,) * 4,
        scratch_shapes=[pltpu.VMEM((TL, 8 * W), F32)],
        compiler_params=params(60),
        cost_estimate=cost(2 * TL * W * 8 * W, 3 * 2**20, TEXT * HD * NH),
        name="text_merge",
    )(tlen, msg, tq, every, proj)


def split_kernel(proj_ref, after_ref, out_ref):
    core = lax.rem(lax.axis_index("tile"), 2)
    mine = pl.ds(pl.multiple_of(core * HALF, 16), HALF)
    for xd in range(4):
        for j in range(2):
            out_ref[xd, :, j * W : (j + 1) * W] = proj_ref[mine, columns(xd, j)]


def split_proj(proj, after_this):
    return pl.pallas_call(
        split_kernel,
        out_shape=jax.ShapeDtypeStruct((4, HALF, 2 * W), BF16),
        in_specs=[VM, ANY],
        out_specs=VM,
        compiler_params=params(60),
        cost_estimate=cost(0, 5 * 2**20),
        name="split_proj",
    )(proj, after_this)


def pack_kernel(k_ref, v_ref, tq_ref, tk_ref, tv_ref, kv_ref, t_ref, buf, sem):
    copies = [
        pltpu.make_async_copy(r, d, sem.at[i])
        for i, (r, d) in enumerate(
            (
                (k_ref, kv_ref.at[pl.ds(0, ROWS)]),
                (v_ref, kv_ref.at[pl.ds(ROWS, ROWS)]),
                (tq_ref, buf.at[0]),
                (tk_ref, buf.at[1]),
                (tv_ref, buf.at[2]),
            )
        )
    ]
    for c in copies:
        c.start()
    for c in copies[2:]:
        c.wait()
    both = jnp.concatenate([buf[i] for i in range(3)], axis=1)
    for i in range(32):
        t_ref[i] = both
    for c in copies[:2]:
        c.wait()


def pack(k, v, tq, tk, tv):
    return pl.pallas_call(
        pack_kernel,
        out_shape=(
            jax.ShapeDtypeStruct((2 * ROWS, W), BF16),
            jax.ShapeDtypeStruct((32, TL, 3 * W), BF16),
        ),
        in_specs=[HBM] * 5,
        out_specs=(VM, VM),
        scratch_shapes=[pltpu.VMEM((3, TL, W), BF16), pltpu.SemaphoreType.DMA((5,))],
        compiler_params=params(60),
        cost_estimate=cost(0, 2 * 2**20),
        name="pack",
    )(k, v, tq, tk, tv)


def after_kernel(x_ref, *rest):
    pass


def after(x, *deps, mib=60):
    return pl.pallas_call(
        after_kernel,
        out_shape=jax.ShapeDtypeStruct(x.shape, x.dtype),
        in_specs=[ANY] * (1 + len(deps)),
        out_specs=ANY,
        input_output_aliases={0: 0},
        compiler_params=params(mib),
        cost_estimate=cost(0, 1),
        name="after",
    )(x, *deps)


def project_kernel(
    a0, a1, a2, a3, w_ref, v_ref, t0, t1, t2, t3, own_ref, away_ref, abuf, wbuf, acc, sem
):
    core = lax.rem(lax.axis_index("tile"), 2)
    me = lax.rem(lax.axis_index("head"), 4)
    copies = []
    for d, a_ref in enumerate((a0, a1, a2, a3)):
        x = lax.rem(me + 4 - d, 4)
        for i, (src, dst) in enumerate(
            (
                (w_ref.at[x], wbuf.at[d, pl.ds(pl.multiple_of(core * HALF, 16), HALF)]),
                (v_ref.at[x], wbuf.at[d, pl.ds(pl.multiple_of((1 - core) * HALF, 16), HALF)]),
                (a_ref, abuf.at[d]),
            )
        ):
            copies.append(pltpu.make_async_copy(src, dst, sem.at[3 * d + i]))
            copies[-1].start()
    t = sum(r[...].astype(F32) for r in (t0, t1, t2, t3))
    t = jnp.concatenate([t, jnp.zeros_like(t)], axis=0)
    own_ref[pl.ds(ROWS, 16), :] = t[:, :W]
    away_ref[pl.ds(ROWS, 16), :] = t[:, W:].astype(BF16)
    for x in range(4):
        for c in copies[3 * x : 3 * x + 3]:
            c.wait()
        o = jnp.dot(abuf[x], wbuf[x], preferred_element_type=F32)
        if x > 0:
            o += acc[...]
        if x < 3:
            acc[...] = o
        else:
            own_ref[:ROWS, :] = o[:, :W]
            away_ref[:ROWS, :] = o[:, W:].astype(BF16)


def project(attn, proj, text):
    return pl.pallas_call(
        project_kernel,
        out_shape=(
            jax.ShapeDtypeStruct((ROWS + 16, W), F32),
            jax.ShapeDtypeStruct((ROWS + 16, W), BF16),
        ),
        in_specs=[ANY] * 6 + [VM] * 4,
        out_specs=(VM, VM),
        scratch_shapes=[
            pltpu.VMEM((4, ROWS, W), BF16),
            pltpu.VMEM((4, W, 2 * W), BF16),
            pltpu.VMEM((ROWS, 2 * W), F32),
            pltpu.SemaphoreType.DMA((12,)),
        ],
        compiler_params=params(24),
        cost_estimate=cost(2 * ROWS * 4 * W * 2 * W, 6 * 2**20),
        name="project",
    )(*attn, *proj, *text)


def add_kernel(own_ref, got_ref, video_ref, text_ref):
    video_ref[...] = (own_ref[:ROWS, :] + got_ref[:ROWS, :].astype(F32)).astype(BF16)
    t = own_ref[pl.ds(ROWS, 16), :] + got_ref[pl.ds(ROWS, 16), :].astype(F32)
    text_ref[...] = t[:TL, :].astype(BF16)


def add_up(own, got):
    return pl.pallas_call(
        add_kernel,
        out_shape=(jax.ShapeDtypeStruct((ROWS, W), BF16), jax.ShapeDtypeStruct((TL, W), BF16)),
        in_specs=[VM, VM],
        out_specs=(VM, VM),
        compiler_params=params(8),
        cost_estimate=cost(0, 2 * 2**20),
        name="add_up",
    )(own, got)


def per_device(
    video_q, video_k, video_v, text_q, text_k, text_v, video_proj, text_proj, window_mask, text_length
):
    kv, text = pack(video_k, video_v, text_q, text_k, text_v)
    far = over_chip(kv)
    up = rows_on(kv, 1)
    dn = rows_on(kv, -1)
    side = other_core(kv)

    every = lax.all_to_all(text, "tile", 0, 0, tiled=True).reshape(TEXT, 3 * W)
    far_up, far_dn = rows_on(far, 1), rows_on(far, -1)
    msg = text_part(every, kv)
    pieces = split_proj(video_proj, side)
    proj = x_swap(pieces)
    up, dn = (after(r, msg, pieces, mib=1) for r in (up, dn))
    side_up, side_dn = other_core(up), other_core(dn)
    acc, m, l = early(
        window_mask, text_length, video_q, every, (kv, up, dn, side, side_up, side_dn)
    )
    msg = after(msg.reshape(32, TL, W + HD), acc)
    got = lax.all_to_all(msg, "tile", 0, 0, tiled=True).reshape(TEXT, W + HD)

    attn = late(window_mask, video_q, (far, far_up, far_dn), acc, m, l)
    attn = [x_on(attn, d) if d else attn for d in range(4)]
    parts = text_merge(text_length, got, text_q, every, text_proj)
    parts = [x_on(p, d) if d else p for d, p in enumerate(parts)]
    own, away = project(attn, (proj, other_core(proj)), parts)
    return add_up(own, z_pair(away))


def solution(mesh):
    both, rows = P("tile", "head"), P("head", None)
    return jax.shard_map(
        per_device,
        mesh=mesh,
        in_specs=(both,) * 6 + (rows, rows, P("tile", None), P()),
        out_specs=(both, both),
        check_vma=False,
    )
```
